512 devices in a mesh: ctx: 64 (over y_lo, z, core), blk: 8 (over x, y_hi).
Axes of the slice: x: 4, y: 4 (y_hi: 2, y_lo: 2; y = y_hi * 2 + y_lo), z: 16, core: 2. Of those that a mesh axis runs over, the one named last changes fastest.
Arguments:
- queries: bfloat16 [128, 2560], P('blk'), may hold values from -6 to 6, as said below
- keys: bfloat16 [196608, 2560], P(('ctx', 'blk')), may hold values from -6 to 6, as said below
- values: bfloat16 [196608, 2560], P(('ctx', 'blk')), may hold values from -8 to 8, as said below
- offset: int32 [1], replicated, may hold values from 147328 to 196480
- lambdas: float32 [10], replicated, may hold values from 0.2 to 0.8
- gain: float32 [2560], replicated, may hold values from 0.5 to 1.5
Outputs:
- normed: bfloat16 [128, 2560], P('blk')
The draws below stay inside these ranges and needn't reach their ends.
Inputs may be any that keep to these rules, and one draw needn't show every extreme that they name: `queries`: entries lie in this range. `keys`: entries lie in this range. `values`: entries lie in this range.
All inputs are finite; a program needn't handle non-finite values.
Results may differ from the reference program's by a relative error of at most 0.01.
Values may be sent and summed in bfloat16 or wider, within the bound.
A program may use at most 64 MiB of HBM per device.

```python
import jax
import jax.numpy as jnp
from jax import lax

H = 10
DH = 128
DV = 256
QCHUNK = 128
CONTEXT = 196608


def draw_queries(key, part):
    key = jax.random.fold_in(key, 11)
    first = jax.random.fold_in(key, 0)
    base = 2.0 * jax.random.normal(first, (QCHUNK, H * 2 * DH), jnp.float32)
    base = jnp.clip(base, -6.0, 6.0)
    return base.astype(jnp.bfloat16)


def draw_keys(key, part):
    key = jax.random.fold_in(key, 12)
    first = jax.random.fold_in(key, 0)
    base = jax.random.normal(first, (CONTEXT, H * 2 * DH), jnp.float32)
    base = jnp.clip(base, -6.0, 6.0)
    return base.astype(jnp.bfloat16)


def draw_values(key, part):
    key = jax.random.fold_in(key, 13)
    first = jax.random.fold_in(key, 0)
    base = jax.random.normal(first, (CONTEXT, H * DV), jnp.float32)
    return jnp.clip(base, -8.0, 8.0).astype(jnp.bfloat16)


def setup_inputs(seed: int = 0) -> dict:
    seeds = jax.random.split(jax.random.key(seed), 7)
    queries = draw_queries(jax.random.fold_in(seeds[6], 71), 0)
    keys = draw_keys(jax.random.fold_in(seeds[6], 71), 0)
    values = draw_values(jax.random.fold_in(seeds[6], 71), 0)
    offset = jax.random.randint(seeds[3], (1,), CONTEXT - QCHUNK - CONTEXT // 4, CONTEXT - QCHUNK + 1).astype(jnp.int32)
    lambdas = jnp.clip(jax.random.uniform(seeds[4], (H,), jnp.float32, 0.2, 0.8), 0.2, 0.8)
    gain = jnp.clip(1.0 + 0.1 * jax.random.normal(seeds[5], (H * DV,), jnp.float32), 0.5, 1.5)
    return dict(queries=queries, keys=keys, values=values, offset=offset, lambdas=lambdas, gain=gain)


def head_output(head, q_four, k_four, v_three, visible, lambdas):
    q_head = lax.dynamic_index_in_dim(q_four, head, 1, keepdims=False)
    k_head = lax.dynamic_index_in_dim(k_four, head, 1, keepdims=False)
    v_head = lax.dynamic_index_in_dim(v_three, head, 1, keepdims=False)
    maps = []
    for half in range(2):
        scores = jnp.dot(q_head[:, half], k_head[:, half].T, preferred_element_type=jnp.float32) * DH ** (-0.5)
        masked = jnp.where(visible, scores, jnp.float32(-1e+30))
        row_max = lax.optimization_barrier(jnp.max(masked, axis=1, keepdims=True))
        expo = jnp.where(visible, jnp.exp(masked - row_max), jnp.float32(0.0))
        totals = lax.optimization_barrier(jnp.sum(expo, axis=1, keepdims=True))
        weighted = jnp.dot(expo.astype(jnp.bfloat16), v_head, preferred_element_type=jnp.float32)
        maps.append(weighted / totals)
    lam_head = lax.dynamic_index_in_dim(lambdas, head, 0, keepdims=False)
    return maps[0] - lam_head * maps[1]

def reference(queries, keys, values, offset, lambdas, gain):
    q_four = queries.reshape(QCHUNK, H, 2, DH)
    k_four = keys.reshape(CONTEXT, H, 2, DH)
    v_three = values.reshape(CONTEXT, H, DV)
    row_pos = offset[0] + jnp.arange(QCHUNK, dtype=jnp.int32)
    key_pos = jnp.arange(CONTEXT, dtype=jnp.int32)
    visible = key_pos[None, :] <= row_pos[:, None]
    attended = lax.map(lambda head: head_output(head, q_four, k_four, v_three, visible, lambdas), jnp.arange(H, dtype=jnp.int32))
    spread = jnp.sqrt(lax.optimization_barrier(jnp.mean(attended * attended, axis=-1, keepdims=True)) + 1e-05)
    normed = attended / spread * gain.reshape(H, 1, DV)
    return normed.transpose(1, 0, 2).reshape(QCHUNK, H * DV).astype(jnp.bfloat16)
```

```python
import functools
import math

import jax
import jax.numpy as jnp
from jax import lax
from jax.experimental import pallas as pl
from jax.experimental.pallas import tpu as pltpu
from jax.sharding import PartitionSpec as P

NX, NY, NZ = 4, 4, 16
CHUNK = 8
HEADS = 5
HALF_Z = NZ // 2
REACH = 3
DH = 128
WIDE = 2 * DH
KEYS = 384
HIDDEN = -1e30
MESH = pl.DeviceIdType.MESH


LAG = 2


def wrap(index, size):
    return jnp.where(index >= size, index - size, index)


def wait_bytes(ref, sem):
    pltpu.make_async_copy(ref, ref, sem).wait()


def send(src, dst, ssem, rsem, to):
    copy = pltpu.make_async_remote_copy(
        src_ref=src, dst_ref=dst, send_sem=ssem, recv_sem=rsem, device_id=to, device_id_type=MESH
    )
    copy.start()
    return copy


def loop(count, body, start=0):
    def step(i, carry):
        body(i)
        return carry

    lax.fori_loop(start, count, step, 0)


def merge_rows(rows):
    top = functools.reduce(jnp.maximum, rows)
    parts = [jnp.exp2(row - top) for row in rows]
    total = functools.reduce(jnp.add, parts)
    inverse = 1.0 / total
    return [part * inverse for part in parts], top + jnp.log2(total)


def column(row):
    lead = row.shape[:-2]
    lane = lax.broadcasted_iota(jnp.int32, lead + (16, 128), len(lead) + 1)
    sub = lax.broadcasted_iota(jnp.int32, lead + (16, 128), len(lead))
    wide = jnp.where(lane == sub, jnp.broadcast_to(row, lead + (16, 128)), 0.0)
    return jnp.sum(wide, axis=-1, keepdims=True)


def weighted(weights, parts):
    acc = None
    for weight, part in zip(weights, parts):
        term = column(weight) * part.astype(jnp.float32)
        acc = term if acc is None else acc + term
    return acc


def kernel(
    offset_hbm, lam_hbm, gain_hbm, q_ref, k_ref, v_ref, out_ref,
    offset_ref, lam_ref, gain_ref,
    kbuf, vbuf, qbuf, bias, obuf, sbuf, part_a, part_b, srow_a, srow_b,
    send_a, send_b, srow2_a, srow2_b, got_a, got_b, sgot_a, sgot_b,
    zsend, zsrow, zbuf, zsbuf, fin,
    small_sem, kl_sem, vl_sem, ql_sem, k_ssem, k_rsem, v_ssem, v_rsem, q_ssem, q_rsem,
    a_ssem, a_rsem, b_ssem, b_rsem, ta_ssem, ta_rsem, tb_ssem, tb_rsem,
    a2_ssem, a2_rsem, b2_ssem, b2_rsem, ta2_ssem, ta2_rsem, tb2_ssem, tb2_rsem,
    z_ssem, z_rsem, zt_ssem, zt_rsem, g_ssem, g_rsem, token_sem,
):
    ctx = lax.axis_index("ctx")
    blk = lax.axis_index("blk")
    core = lax.rem(ctx, 2)
    z = lax.rem(ctx // 2, NZ)
    y_lo = ctx // (2 * NZ)
    x = blk // 2
    y = lax.rem(blk, 2) * 2 + y_lo
    other = 1 - core
    y_hi = lax.rem(blk, 2)
    xs = [wrap(x + d, NX) for d in range(1, NX)]
    ys = [wrap(y + d, NY) for d in range(1, NY)]
    beside = (ctx + other - core, blk)
    pair = (ctx + 2 * NZ * (1 - 2 * y_lo), blk)
    x_line = [(ctx, xx * 2 + y_hi) for xx in xs]
    y_line = [((lax.rem(yy, 2) * NZ + z) * 2 + core, x * 2 + yy // 2) for yy in ys]
    mirror = [(pair[0], xx * 2 + 1 - y_hi) for xx in [x] + xs]
    z_base = y_lo * 2 * NZ + core

    def z_line(d):
        return (z_base + 2 * wrap(z + d, NZ), blk)

    steps = (0, other - core, 2 * NZ * (1 - 2 * y_lo), 2 * NZ * (1 - 2 * y_lo) + other - core)

    def column_at(i, zz):
        return (z_base + steps[i] + 2 * zz, blk)

    def cols(which, head, count=1):
        return pl.ds(pl.multiple_of(which * (HEADS * WIDE) + head * WIDE, WIDE), count * WIDE)

    barrier = pltpu.get_barrier_semaphore()

    def greet(to):
        pl.semaphore_signal(barrier, inc=1, device_id=to, device_id_type=MESH)

    near = [beside] + x_line + y_line + mirror[1:] + [z_line(1), z_line(NZ - 1), column_at(3, z)]
    for to in near:
        greet(to)

    def own_copies(h):
        return (
            pltpu.make_async_copy(k_ref.at[:, cols(core, h)], kbuf.at[0, h], kl_sem.at[h]),
            pltpu.make_async_copy(v_ref.at[:, cols(core, h)], vbuf.at[0, h], vl_sem.at[h]),
        )

    def start_own(h):
        for copy in own_copies(h):
            copy.start()

    own_q = pltpu.make_async_copy(q_ref.at[:, cols(core, 0, HEADS)], qbuf.at[blk], ql_sem)
    own_q.start()
    loop(HEADS, start_own)
    small = [
        pltpu.make_async_copy(offset_hbm, offset_ref, small_sem.at[0]),
        pltpu.make_async_copy(lam_hbm, lam_ref, small_sem.at[1]),
        pltpu.make_async_copy(gain_hbm, gain_ref, small_sem.at[2]),
    ]
    for copy in small:
        copy.start()
    pl.semaphore_wait(barrier, len(near))

    def pushes(h):
        return (
            pltpu.make_async_remote_copy(
                src_ref=k_ref.at[:, cols(other, h)], dst_ref=kbuf.at[1, h], send_sem=k_ssem.at[h],
                recv_sem=k_rsem.at[h], device_id=beside, device_id_type=MESH,
            ),
            pltpu.make_async_remote_copy(
                src_ref=v_ref.at[:, cols(other, h)], dst_ref=vbuf.at[1, h], send_sem=v_ssem.at[h],
                recv_sem=v_rsem.at[h], device_id=beside, device_id_type=MESH,
            ),
        )

    def push(h):
        for copy in pushes(h):
            copy.start()

    def queries_of(h):
        return qbuf.at[pl.ds(0, 7), :, cols(0, h)]

    def push_head(h):
        mine = q_ref.at[:, cols(core, h)]
        for to in mirror + x_line:
            send(mine, qbuf.at[blk, :, cols(0, h)], q_ssem.at[h], q_rsem.at[h], to)
        push(h)

    loop(HEADS, push_head)

    def token(step):
        for d in (2**step, NZ - 2**step):
            pl.semaphore_signal(token_sem.at[step], inc=1, device_id=z_line(d), device_id_type=MESH)

    token(0)

    row = lax.broadcasted_iota(jnp.int32, (32 * CHUNK, KEYS), 0)
    pos = lax.broadcasted_iota(jnp.int32, (32 * CHUNK, KEYS), 1)
    ahead = pos - (lax.shift_right_logical(row, 4) * CHUNK + (row & (CHUNK - 1)))
    small[0].wait()
    for s in range(2):
        owner = ctx if s == 0 else ctx + other - core
        start = (owner * 8 + blk) * KEYS
        bias[s] = jnp.where(ahead <= offset_ref[0] - start, 0.0, HIDDEN)

    scale = DH ** (-0.5) * math.log2(math.e)

    def attend(h):
        own_k, own_v = own_copies(h)
        wait_bytes(queries_of(h), q_rsem.at[h])
        own_k.wait()
        wait_bytes(kbuf.at[1, h], k_rsem.at[h])
        lane3 = lax.broadcasted_iota(jnp.int32, (16, CHUNK, WIDE), 2)
        q = qbuf[:, :, cols(0, h)].astype(jnp.float32).reshape(16, CHUNK, WIDE)
        low = jnp.where(lane3 < DH, q, 0.0)
        high = jnp.where(lane3 >= DH, q, 0.0)
        both = jnp.concatenate([low, high], axis=1).reshape(256, WIDE).astype(jnp.bfloat16)
        scores = []
        for s in range(2):
            dot = lax.dot_general(
                both, kbuf[s, h], (((1,), (1,)), ((), ())), preferred_element_type=jnp.float32
            )
            scores.append(dot * scale + bias[s])
        top = jnp.max(jnp.maximum(scores[0], scores[1]), axis=1, keepdims=True)
        expo = [jnp.exp2(t - top) for t in scores]
        total = jnp.sum(expo[0] + expo[1], axis=1, keepdims=True)
        own_v.wait()
        wait_bytes(vbuf.at[1, h], v_rsem.at[h])
        out = sum(
            jnp.dot(expo[s].astype(jnp.bfloat16), vbuf[s, h], preferred_element_type=jnp.float32)
            for s in range(2)
        )
        out = (out * (1.0 / total)).reshape(NX, NY, 16, WIDE).astype(jnp.bfloat16)
        obuf[h, 0] = out[..., :DH]
        obuf[h, 1] = out[..., DH:]
        stat_lane = lax.broadcasted_iota(jnp.int32, (16, 16, 128), 2)
        stat_sub = lax.broadcasted_iota(jnp.int32, (16, 16, 128), 1)
        stat = jnp.broadcast_to((top + jnp.log2(total)).reshape(16, 16, 1), (16, 16, 128))
        spread = jnp.where(stat_lane == stat_sub, stat, 0.0)
        sbuf[h] = jnp.sum(spread, axis=1, keepdims=True).reshape(NX, NY, 1, 128)
        for d in range(NX - 1):
            send(sbuf.at[h, xs[d]], srow_a.at[h, d], ta_ssem.at[h], ta_rsem.at[h], x_line[d])
            send(sbuf.at[h, :, ys[d]], srow_b.at[h, d], tb_ssem.at[h], tb_rsem.at[h], y_line[d])
        for d in range(NX - 1):
            send(obuf.at[h, 0, xs[d]], part_a.at[h, d], a_ssem.at[h], a_rsem.at[h], x_line[d])
            send(obuf.at[h, 1, :, ys[d]], part_b.at[h, d], b_ssem.at[h], b_rsem.at[h], y_line[d])

    def first_step(h):
        wait_bytes(srow_a.at[h], ta_rsem.at[h])
        weights_a, whole_a = merge_rows([sbuf[h, x]] + [srow_a[h, d] for d in range(NX - 1)])
        srow2_a[h] = whole_a
        wait_bytes(srow_b.at[h], tb_rsem.at[h])
        weights_b, whole_b = merge_rows([sbuf[h, :, y]] + [srow_b[h, d] for d in range(NY - 1)])
        srow2_b[h] = whole_b
        for d in range(NX - 1):
            send(srow2_a.at[h, ys[d]], sgot_a.at[h, d], ta2_ssem.at[h], ta2_rsem.at[h], y_line[d])
            send(srow2_b.at[h, xs[d]], sgot_b.at[h, d], tb2_ssem.at[h], tb2_rsem.at[h], x_line[d])
        wait_bytes(part_a.at[h], a_rsem.at[h])
        parts = [obuf[h, 0, x]] + [part_a[h, d] for d in range(NX - 1)]
        send_a[h] = weighted(weights_a, parts).astype(jnp.bfloat16)
        wait_bytes(part_b.at[h], b_rsem.at[h])
        parts = [obuf[h, 1, :, y]] + [part_b[h, d] for d in range(NY - 1)]
        send_b[h] = weighted(weights_b, parts).astype(jnp.bfloat16)
        for d in range(NX - 1):
            send(send_a.at[h, ys[d]], got_a.at[h, d], a2_ssem.at[h], a2_rsem.at[h], y_line[d])
            send(send_b.at[h, xs[d]], got_b.at[h, d], b2_ssem.at[h], b2_rsem.at[h], x_line[d])

    def owner_of(h):
        return lax.rem(3 * h + HALF_Z - core, HALF_Z)

    def second_step(h):
        wait_bytes(sgot_a.at[h], ta2_rsem.at[h])
        wait_bytes(sgot_b.at[h], tb2_rsem.at[h])
        weights_a, whole_a = merge_rows([srow2_a[h, y]] + [sgot_a[h, d] for d in range(NY - 1)])
        weights_b, _ = merge_rows([srow2_b[h, x]] + [sgot_b[h, d] for d in range(NX - 1)])
        zsrow[h] = whole_a
        wait_bytes(got_a.at[h], a2_rsem.at[h])
        parts = [send_a[h, y]] + [got_a[h, d] for d in range(NY - 1)]
        zsend[h, :, :DH] = weighted(weights_a, parts).astype(jnp.bfloat16)
        wait_bytes(got_b.at[h], b2_rsem.at[h])
        parts = [send_b[h, x]] + [got_b[h, d] for d in range(NX - 1)]
        zsend[h, :, DH:] = weighted(weights_b, parts).astype(jnp.bfloat16)
        for i in range(2):
            owner = owner_of(h) + i * HALF_Z
            gap = wrap(owner - z + NZ, NZ)

            @pl.when(gap != 0)
            def _():
                to = (z_base + 2 * owner, blk)
                send(zsrow.at[h], zsbuf.at[gap - 1], zt_ssem.at[h, i], zt_rsem, to)
                send(zsend.at[h], zbuf.at[gap - 1], z_ssem.at[h, i], z_rsem, to)

    def turn_of(i):
        @pl.when(i < HEADS)
        def _():
            attend(i)

        for step in range(2):

            @pl.when(i == LAG + step)
            def _():
                pl.semaphore_wait(token_sem.at[step], 2)
                token(step + 1)

        @pl.when(i == 2 * LAG)
        def _():
            pl.semaphore_wait(token_sem.at[2], 2)

        @pl.when(jnp.logical_and(i >= LAG, i < HEADS + LAG))
        def _():
            first_step(i - LAG)

        @pl.when(i >= 2 * LAG)
        def _():
            second_step(i - 2 * LAG)

    own_q.wait()
    loop(HEADS + 2 * LAG, turn_of)

    mine = lax.rem(3 * (z + core), HALF_Z)
    is_owner = mine < HEADS
    all_tiles = 4 * HEADS
    small[1].wait()
    small[2].wait()

    @pl.when(is_owner)
    def _():
        wait_bytes(zsbuf, zt_rsem)
        weights, _ = merge_rows([zsrow[mine]] + [zsbuf[d] for d in range(NZ - 1)])
        wait_bytes(zbuf, z_rsem)
        acc = weighted(weights, [zsend[mine]] + [zbuf[d] for d in range(NZ - 1)])
        head = core * HEADS + mine
        attended = acc[:CHUNK] - lam_ref[head] * acc[CHUNK:]
        spread = jnp.sqrt(jnp.mean(attended * attended, axis=-1, keepdims=True) + 1e-5)
        normed = attended / spread * gain_ref[cols(0, head)].reshape(1, WIDE)
        halves = jnp.concatenate([normed[:, :DH], normed[:, DH:]], axis=0)
        slot = (y_lo * 2 + core) * HEADS + mine
        fin[slot] = halves.astype(jnp.bfloat16)
        tile = fin.at[slot]

        def give(d):
            zz = wrap(wrap(z + d + NZ - REACH, 2 * NZ), NZ)
            for i in range(1, 4):
                send(tile, tile, g_ssem.at[i], g_rsem, column_at(i, zz))

            @pl.when(zz != z)
            def _():
                send(tile, tile, g_ssem.at[0], g_rsem, column_at(0, zz))

        loop(HALF_Z, give)
        wait_bytes(fin.at[pl.ds(0, all_tiles - 1)], g_rsem)

    @pl.when(jnp.logical_not(is_owner))
    def _():
        wait_bytes(fin, g_rsem)

    def assemble(h):
        for c in range(2):
            first = fin[c * HEADS + h].astype(jnp.float32)
            second = fin[(2 + c) * HEADS + h].astype(jnp.float32)
            low = jnp.concatenate([first[:CHUNK], second[:CHUNK]], axis=0)
            high = jnp.concatenate([first[CHUNK:], second[CHUNK:]], axis=0)
            out_ref[:, cols(c, h)] = jnp.concatenate([low, high], axis=1).astype(jnp.bfloat16)

    loop(HEADS, assemble)

    def left(h):
        for copy in pushes(h):
            copy.wait_send()
        wait_bytes(queries_of(h), q_ssem.at[h])
        for part, sem in (
            (part_a, a_ssem), (part_b, b_ssem), (srow_a, ta_ssem), (srow_b, tb_ssem),
            (got_a, a2_ssem), (got_b, b2_ssem), (sgot_a, ta2_ssem), (sgot_b, tb2_ssem),
        ):
            wait_bytes(part.at[h], sem.at[h])

        for i in range(2):

            @pl.when(owner_of(h) + i * HALF_Z != z)
            def _():
                wait_bytes(zsend.at[h], z_ssem.at[h, i])
                wait_bytes(zsrow.at[h], zt_ssem.at[h, i])

    loop(HEADS, left)
    @pl.when(is_owner)
    def _():
        wait_bytes(fin.at[pl.ds(0, HALF_Z - 1)], g_ssem.at[0])
        for i in range(1, 4):
            wait_bytes(fin.at[pl.ds(0, HALF_Z)], g_ssem.at[i])


def per_device(queries, keys, values, offset, lambdas, gain):
    row_count, width = queries.shape
    bf16, f32 = jnp.bfloat16, jnp.float32
    dma = pltpu.SemaphoreType.DMA
    heads = dma((HEADS,))
    hbm = pl.BlockSpec(memory_space=pltpu.HBM)
    vmem = pl.BlockSpec(memory_space=pltpu.VMEM)
    return pl.pallas_call(
        kernel,
        out_shape=jax.ShapeDtypeStruct((row_count, width), bf16),
        in_specs=[hbm] * 6,
        out_specs=vmem,
        scratch_shapes=[
            pltpu.SMEM((1,), jnp.int32),
            pltpu.SMEM(lambdas.shape, f32),
            pltpu.VMEM(gain.shape, f32),
            pltpu.VMEM((2, HEADS, KEYS, WIDE), bf16),
            pltpu.VMEM((2, HEADS, KEYS, WIDE), bf16),
            pltpu.VMEM((8, 16, HEADS * WIDE), bf16),
            pltpu.VMEM((2, 256, KEYS), f32),
            pltpu.VMEM((HEADS, 2, NX, NY, 16, DH), bf16),
            pltpu.VMEM((HEADS, NX, NY, 1, 128), f32),
            pltpu.VMEM((HEADS, NX - 1, NY, 16, DH), bf16),
            pltpu.VMEM((HEADS, NY - 1, NX, 16, DH), bf16),
            pltpu.VMEM((HEADS, NX - 1, NY, 1, 128), f32),
            pltpu.VMEM((HEADS, NY - 1, NX, 1, 128), f32),
            pltpu.VMEM((HEADS, NY, 16, DH), bf16),
            pltpu.VMEM((HEADS, NX, 16, DH), bf16),
            pltpu.VMEM((HEADS, NY, 1, 128), f32),
            pltpu.VMEM((HEADS, NX, 1, 128), f32),
            pltpu.VMEM((HEADS, NY - 1, 16, DH), bf16),
            pltpu.VMEM((HEADS, NX - 1, 16, DH), bf16),
            pltpu.VMEM((HEADS, NY - 1, 1, 128), f32),
            pltpu.VMEM((HEADS, NX - 1, 1, 128), f32),
            pltpu.VMEM((HEADS, 16, WIDE), bf16),
            pltpu.VMEM((HEADS, 1, 128), f32),
            pltpu.VMEM((NZ - 1, 16, WIDE), bf16),
            pltpu.VMEM((NZ - 1, 1, 128), f32),
            pltpu.VMEM((4 * HEADS, 16, DH), bf16),
            dma((3,)), heads, heads, dma,
            heads, heads, heads, heads, heads, heads,
            heads, heads, heads, heads, heads, heads, heads, heads,
            heads, heads, heads, heads, heads, heads, heads, heads,
            dma((HEADS, 2)), dma, dma((HEADS, 2)), dma, dma((4,)), dma,
            pltpu.SemaphoreType.REGULAR((3,)),
        ],
        compiler_params=pltpu.CompilerParams(
            collective_id=0, has_side_effects=True, vmem_limit_bytes=64 * 1024 * 1024
        ),
        cost_estimate=pl.CostEstimate(flops=800_000_000, bytes_accessed=8_000_000, transcendentals=1_000_000),
    )(offset, lambdas, gain, queries, keys, values)


def solution(mesh):
    return jax.shard_map(
        per_device,
        mesh=mesh,
        in_specs=(P("blk", None), P(("ctx", "blk"), None), P(("ctx", "blk"), None), P(), P(), P()),
        out_specs=P("blk", None),
        check_vma=False,
    )
```

```python
import functools
import math

import jax
import jax.numpy as jnp
from jax import lax
from jax.experimental import pallas as pl
from jax.experimental.pallas import tpu as pltpu
from jax.sharding import PartitionSpec as P

NX, NY, NZ = 4, 4, 16
CHUNK = 8
HEADS = 5
HALF_Z = NZ // 2
REACH = 3
DH = 128
WIDE = 2 * DH
KEYS = 384
HIDDEN = -1e30
MESH = pl.DeviceIdType.MESH


LAG = 2


def wrap(index, size):
    return jnp.where(index >= size, index - size, index)


def wait_bytes(ref, sem):
    pltpu.make_async_copy(ref, ref, sem).wait()


def send(src, dst, ssem, rsem, to):
    copy = pltpu.make_async_remote_copy(
        src_ref=src, dst_ref=dst, send_sem=ssem, recv_sem=rsem, device_id=to, device_id_type=MESH
    )
    copy.start()
    return copy


def loop(count, body, start=0):
    def step(i, carry):
        body(i)
        return carry

    lax.fori_loop(start, count, step, 0)


def merge_rows(rows):
    top = functools.reduce(jnp.maximum, rows)
    parts = [jnp.exp2(row - top) for row in rows]
    total = functools.reduce(jnp.add, parts)
    inverse = 1.0 / total
    return [part * inverse for part in parts], top + jnp.log2(total)


def column(row):
    lead = row.shape[:-2]
    lane = lax.broadcasted_iota(jnp.int32, lead + (16, 128), len(lead) + 1)
    sub = lax.broadcasted_iota(jnp.int32, lead + (16, 128), len(lead))
    wide = jnp.where(lane == sub, jnp.broadcast_to(row, lead + (16, 128)), 0.0)
    return jnp.sum(wide, axis=-1, keepdims=True)


def weighted(weights, parts):
    acc = None
    for weight, part in zip(weights, parts):
        term = column(weight) * part.astype(jnp.float32)
        acc = term if acc is None else acc + term
    return acc


def kernel(
    offset_hbm, lam_hbm, gain_hbm, q_ref, k_ref, v_ref, out_ref,
    offset_ref, lam_ref, gain_ref,
    kbuf, vbuf, qbuf, bias, tall, scores, expo, inverse, maps, obuf, sbuf, part_a, part_b, srow_a, srow_b,
    send_a, send_b, srow2_a, srow2_b, got_a, got_b, sgot_a, sgot_b,
    zsend, zsrow, zbuf, zsbuf, fin,
    small_sem, kl_sem, vl_sem, ql_sem, k_ssem, k_rsem, v_ssem, v_rsem, q_ssem, q_rsem,
    a_ssem, a_rsem, b_ssem, b_rsem, ta_ssem, ta_rsem, tb_ssem, tb_rsem,
    a2_ssem, a2_rsem, b2_ssem, b2_rsem, ta2_ssem, ta2_rsem, tb2_ssem, tb2_rsem,
    z_ssem, z_rsem, zt_ssem, zt_rsem, g_ssem, g_rsem, token_sem,
):
    ctx = lax.axis_index("ctx")
    blk = lax.axis_index("blk")
    core = lax.rem(ctx, 2)
    z = lax.rem(ctx // 2, NZ)
    y_lo = ctx // (2 * NZ)
    x = blk // 2
    y = lax.rem(blk, 2) * 2 + y_lo
    other = 1 - core
    y_hi = lax.rem(blk, 2)
    xs = [wrap(x + d, NX) for d in range(1, NX)]
    ys = [wrap(y + d, NY) for d in range(1, NY)]
    beside = (ctx + other - core, blk)
    pair = (ctx + 2 * NZ * (1 - 2 * y_lo), blk)
    x_line = [(ctx, xx * 2 + y_hi) for xx in xs]
    y_line = [((lax.rem(yy, 2) * NZ + z) * 2 + core, x * 2 + yy // 2) for yy in ys]
    mirror = [(pair[0], xx * 2 + 1 - y_hi) for xx in [x] + xs]
    z_base = y_lo * 2 * NZ + core

    def z_line(d):
        return (z_base + 2 * wrap(z + d, NZ), blk)

    steps = (0, other - core, 2 * NZ * (1 - 2 * y_lo), 2 * NZ * (1 - 2 * y_lo) + other - core)

    def column_at(i, zz):
        return (z_base + steps[i] + 2 * zz, blk)

    def cols(which, head, count=1):
        return pl.ds(pl.multiple_of(which * (HEADS * WIDE) + head * WIDE, WIDE), count * WIDE)

    barrier = pltpu.get_barrier_semaphore()

    def greet(to):
        pl.semaphore_signal(barrier, inc=1, device_id=to, device_id_type=MESH)

    near = [beside] + x_line + y_line + mirror[1:] + [z_line(1), z_line(NZ - 1), column_at(3, z)]
    for to in near:
        greet(to)

    def own_copies(h):
        return (
            pltpu.make_async_copy(k_ref.at[:, cols(core, h)], kbuf.at[h, pl.ds(0, KEYS)], kl_sem.at[h]),
            pltpu.make_async_copy(v_ref.at[:, cols(core, h)], vbuf.at[h, pl.ds(0, KEYS)], vl_sem.at[h]),
        )

    def start_own(h):
        for copy in own_copies(h):
            copy.start()

    own_q = pltpu.make_async_copy(q_ref.at[:, cols(core, 0, HEADS)], qbuf.at[blk], ql_sem)
    own_q.start()
    loop(HEADS, start_own)
    small = [
        pltpu.make_async_copy(offset_hbm, offset_ref, small_sem.at[0]),
        pltpu.make_async_copy(lam_hbm, lam_ref, small_sem.at[1]),
        pltpu.make_async_copy(gain_hbm, gain_ref, small_sem.at[2]),
    ]
    for copy in small:
        copy.start()
    pl.semaphore_wait(barrier, len(near))

    def pushes(h):
        return (
            pltpu.make_async_remote_copy(
                src_ref=k_ref.at[:, cols(other, h)], dst_ref=kbuf.at[h, pl.ds(KEYS, KEYS)], send_sem=k_ssem.at[h],
                recv_sem=k_rsem.at[h], device_id=beside, device_id_type=MESH,
            ),
            pltpu.make_async_remote_copy(
                src_ref=v_ref.at[:, cols(other, h)], dst_ref=vbuf.at[h, pl.ds(KEYS, KEYS)], send_sem=v_ssem.at[h],
                recv_sem=v_rsem.at[h], device_id=beside, device_id_type=MESH,
            ),
        )

    def push(h):
        for copy in pushes(h):
            copy.start()

    def queries_of(h):
        return qbuf.at[pl.ds(0, 7), :, cols(0, h)]

    def push_head(h):
        mine = q_ref.at[:, cols(core, h)]
        for to in mirror + x_line:
            send(mine, qbuf.at[blk, :, cols(0, h)], q_ssem.at[h], q_rsem.at[h], to)
        push(h)

    loop(HEADS, push_head)

    def token(step):
        for d in (2**step, NZ - 2**step):
            pl.semaphore_signal(token_sem.at[step], inc=1, device_id=z_line(d), device_id_type=MESH)

    token(0)

    row = lax.broadcasted_iota(jnp.int32, (32 * CHUNK, KEYS), 0)
    pos = lax.broadcasted_iota(jnp.int32, (32 * CHUNK, KEYS), 1)
    ahead = pos - (lax.shift_right_logical(row, 4) * CHUNK + (row & (CHUNK - 1)))
    small[0].wait()
    for s in range(2):
        owner = ctx if s == 0 else ctx + other - core
        start = (owner * 8 + blk) * KEYS
        bias[:, s * KEYS : s * KEYS + KEYS] = jnp.where(ahead <= offset_ref[0] - start, 0.0, HIDDEN)

    scale = DH ** (-0.5) * math.log2(math.e)

    def attend(h):
        own_k, own_v = own_copies(h)
        wait_bytes(queries_of(h), q_rsem.at[h])
        blocks = [slice(32 * b, 32 * b + 32) for b in range(8)]
        lane = lax.broadcasted_iota(jnp.int32, (2, CHUNK, WIDE), 2)
        for b, rows in enumerate(blocks):
            q = qbuf[b, :, cols(0, h)].astype(jnp.float32).reshape(2, CHUNK, WIDE)
            both = jnp.concatenate([jnp.where(lane < DH, q, 0.0), jnp.where(lane >= DH, q, 0.0)], axis=1)
            tall[rows] = both.reshape(32, WIDE).astype(jnp.bfloat16)
        own_k.wait()
        wait_bytes(kbuf.at[h, pl.ds(KEYS, KEYS)], k_rsem.at[h])
        scores[...] = lax.dot_general(
            tall[...], kbuf[h], (((1,), (1,)), ((), ())), preferred_element_type=jnp.float32
        )
        stat_lane = lax.broadcasted_iota(jnp.int32, (2, 16, 128), 2)
        stat_sub = lax.broadcasted_iota(jnp.int32, (2, 16, 128), 1)
        for b, rows in enumerate(blocks):
            score = scores[rows] * scale + bias[rows]
            top = jnp.max(score, axis=1, keepdims=True)
            e = jnp.exp2(score - top)
            total = jnp.sum(e, axis=1, keepdims=True)
            expo[rows] = e.astype(jnp.bfloat16)
            inverse[rows] = jnp.broadcast_to(1.0 / total, (32, 128))
            stat = jnp.broadcast_to((top + jnp.log2(total)).reshape(2, 16, 1), (2, 16, 128))
            stat = jnp.where(stat_lane == stat_sub, stat, 0.0)
            sbuf[h, b // 2, (b % 2) * 2 : (b % 2) * 2 + 2] = jnp.sum(stat, axis=1, keepdims=True)
        own_v.wait()
        wait_bytes(vbuf.at[h, pl.ds(KEYS, KEYS)], v_rsem.at[h])
        maps[...] = jnp.dot(expo[...], vbuf[h], preferred_element_type=jnp.float32)
        for b, rows in enumerate(blocks):
            for half in range(2):
                part = maps[rows, half * DH : half * DH + DH] * inverse[rows]
                part = part.reshape(2, 16, DH).astype(jnp.bfloat16)
                obuf[h, half, b // 2, (b % 2) * 2 : (b % 2) * 2 + 2] = part
        for d in range(NX - 1):
            send(sbuf.at[h, xs[d]], srow_a.at[h, d], ta_ssem.at[h], ta_rsem.at[h], x_line[d])
            send(sbuf.at[h, :, ys[d]], srow_b.at[h, d], tb_ssem.at[h], tb_rsem.at[h], y_line[d])
        for d in range(NX - 1):
            send(obuf.at[h, 0, xs[d]], part_a.at[h, d], a_ssem.at[h], a_rsem.at[h], x_line[d])
            send(obuf.at[h, 1, :, ys[d]], part_b.at[h, d], b_ssem.at[h], b_rsem.at[h], y_line[d])

    def first_step(h):
        wait_bytes(srow_a.at[h], ta_rsem.at[h])
        weights_a, whole_a = merge_rows([sbuf[h, x]] + [srow_a[h, d] for d in range(NX - 1)])
        srow2_a[h] = whole_a
        wait_bytes(srow_b.at[h], tb_rsem.at[h])
        weights_b, whole_b = merge_rows([sbuf[h, :, y]] + [srow_b[h, d] for d in range(NY - 1)])
        srow2_b[h] = whole_b
        for d in range(NX - 1):
            send(srow2_a.at[h, ys[d]], sgot_a.at[h, d], ta2_ssem.at[h], ta2_rsem.at[h], y_line[d])
            send(srow2_b.at[h, xs[d]], sgot_b.at[h, d], tb2_ssem.at[h], tb2_rsem.at[h], x_line[d])
        wait_bytes(part_a.at[h], a_rsem.at[h])
        parts = [obuf[h, 0, x]] + [part_a[h, d] for d in range(NX - 1)]
        send_a[h] = weighted(weights_a, parts).astype(jnp.bfloat16)
        wait_bytes(part_b.at[h], b_rsem.at[h])
        parts = [obuf[h, 1, :, y]] + [part_b[h, d] for d in range(NY - 1)]
        send_b[h] = weighted(weights_b, parts).astype(jnp.bfloat16)
        for d in range(NX - 1):
            send(send_a.at[h, ys[d]], got_a.at[h, d], a2_ssem.at[h], a2_rsem.at[h], y_line[d])
            send(send_b.at[h, xs[d]], got_b.at[h, d], b2_ssem.at[h], b2_rsem.at[h], x_line[d])

    def owner_of(h):
        return lax.rem(3 * h + HALF_Z - core, HALF_Z)

    def second_step(h):
        wait_bytes(sgot_a.at[h], ta2_rsem.at[h])
        wait_bytes(sgot_b.at[h], tb2_rsem.at[h])
        weights_a, whole_a = merge_rows([srow2_a[h, y]] + [sgot_a[h, d] for d in range(NY - 1)])
        weights_b, _ = merge_rows([srow2_b[h, x]] + [sgot_b[h, d] for d in range(NX - 1)])
        zsrow[h] = whole_a
        wait_bytes(got_a.at[h], a2_rsem.at[h])
        parts = [send_a[h, y]] + [got_a[h, d] for d in range(NY - 1)]
        zsend[h, :, :DH] = weighted(weights_a, parts).astype(jnp.bfloat16)
        wait_bytes(got_b.at[h], b2_rsem.at[h])
        parts = [send_b[h, x]] + [got_b[h, d] for d in range(NX - 1)]
        zsend[h, :, DH:] = weighted(weights_b, parts).astype(jnp.bfloat16)
        for i in range(2):
            owner = owner_of(h) + i * HALF_Z
            gap = wrap(owner - z + NZ, NZ)

            @pl.when(gap != 0)
            def _():
                to = (z_base + 2 * owner, blk)
                send(zsrow.at[h], zsbuf.at[gap - 1], zt_ssem.at[h, i], zt_rsem, to)
                send(zsend.at[h], zbuf.at[gap - 1], z_ssem.at[h, i], z_rsem, to)

    def turn_of(i):
        @pl.when(i < HEADS)
        def _():
            attend(i)

        for step in range(2):

            @pl.when(i == LAG + step)
            def _():
                pl.semaphore_wait(token_sem.at[step], 2)
                token(step + 1)

        @pl.when(i == 2 * LAG)
        def _():
            pl.semaphore_wait(token_sem.at[2], 2)

        @pl.when(jnp.logical_and(i >= LAG, i < HEADS + LAG))
        def _():
            first_step(i - LAG)

        @pl.when(i >= 2 * LAG)
        def _():
            second_step(i - 2 * LAG)

    own_q.wait()
    loop(HEADS + 2 * LAG, turn_of)

    mine = lax.rem(3 * (z + core), HALF_Z)
    is_owner = mine < HEADS
    all_tiles = 4 * HEADS
    small[1].wait()
    small[2].wait()

    @pl.when(is_owner)
    def _():
        wait_bytes(zsbuf, zt_rsem)
        weights, _ = merge_rows([zsrow[mine]] + [zsbuf[d] for d in range(NZ - 1)])
        wait_bytes(zbuf, z_rsem)
        acc = weighted(weights, [zsend[mine]] + [zbuf[d] for d in range(NZ - 1)])
        head = core * HEADS + mine
        attended = acc[:CHUNK] - lam_ref[head] * acc[CHUNK:]
        spread = jnp.sqrt(jnp.mean(attended * attended, axis=-1, keepdims=True) + 1e-5)
        normed = attended / spread * gain_ref[cols(0, head)].reshape(1, WIDE)
        halves = jnp.concatenate([normed[:, :DH], normed[:, DH:]], axis=0)
        slot = (y_lo * 2 + core) * HEADS + mine
        fin[slot] = halves.astype(jnp.bfloat16)
        tile = fin.at[slot]

        def give(d):
            zz = wrap(wrap(z + d + NZ - REACH, 2 * NZ), NZ)
            for i in range(1, 4):
                send(tile, tile, g_ssem.at[i], g_rsem, column_at(i, zz))

            @pl.when(zz != z)
            def _():
                send(tile, tile, g_ssem.at[0], g_rsem, column_at(0, zz))

        loop(HALF_Z, give)
        wait_bytes(fin.at[pl.ds(0, all_tiles - 1)], g_rsem)

    @pl.when(jnp.logical_not(is_owner))
    def _():
        wait_bytes(fin, g_rsem)

    def assemble(h):
        for c in range(2):
            first = fin[c * HEADS + h].astype(jnp.float32)
            second = fin[(2 + c) * HEADS + h].astype(jnp.float32)
            low = jnp.concatenate([first[:CHUNK], second[:CHUNK]], axis=0)
            high = jnp.concatenate([first[CHUNK:], second[CHUNK:]], axis=0)
            out_ref[:, cols(c, h)] = jnp.concatenate([low, high], axis=1).astype(jnp.bfloat16)

    loop(HEADS, assemble)

    def left(h):
        for copy in pushes(h):
            copy.wait_send()
        wait_bytes(queries_of(h), q_ssem.at[h])
        for part, sem in (
            (part_a, a_ssem), (part_b, b_ssem), (srow_a, ta_ssem), (srow_b, tb_ssem),
            (got_a, a2_ssem), (got_b, b2_ssem), (sgot_a, ta2_ssem), (sgot_b, tb2_ssem),
        ):
            wait_bytes(part.at[h], sem.at[h])

        for i in range(2):

            @pl.when(owner_of(h) + i * HALF_Z != z)
            def _():
                wait_bytes(zsend.at[h], z_ssem.at[h, i])
                wait_bytes(zsrow.at[h], zt_ssem.at[h, i])

    loop(HEADS, left)
    @pl.when(is_owner)
    def _():
        wait_bytes(fin.at[pl.ds(0, HALF_Z - 1)], g_ssem.at[0])
        for i in range(1, 4):
            wait_bytes(fin.at[pl.ds(0, HALF_Z)], g_ssem.at[i])


def per_device(queries, keys, values, offset, lambdas, gain):
    row_count, width = queries.shape
    bf16, f32 = jnp.bfloat16, jnp.float32
    dma = pltpu.SemaphoreType.DMA
    heads = dma((HEADS,))
    hbm = pl.BlockSpec(memory_space=pltpu.HBM)
    vmem = pl.BlockSpec(memory_space=pltpu.VMEM)
    return pl.pallas_call(
        kernel,
        out_shape=jax.ShapeDtypeStruct((row_count, width), bf16),
        in_specs=[hbm] * 6,
        out_specs=vmem,
        scratch_shapes=[
            pltpu.SMEM((1,), jnp.int32),
            pltpu.SMEM(lambdas.shape, f32),
            pltpu.VMEM(gain.shape, f32),
            pltpu.VMEM((HEADS, 2 * KEYS, WIDE), bf16),
            pltpu.VMEM((HEADS, 2 * KEYS, WIDE), bf16),
            pltpu.VMEM((8, 16, HEADS * WIDE), bf16),
            pltpu.VMEM((256, 2 * KEYS), f32),
            pltpu.VMEM((256, WIDE), bf16),
            pltpu.VMEM((256, 2 * KEYS), f32),
            pltpu.VMEM((256, 2 * KEYS), bf16),
            pltpu.VMEM((256, 128), f32),
            pltpu.VMEM((256, WIDE), f32),
            pltpu.VMEM((HEADS, 2, NX, NY, 16, DH), bf16),
            pltpu.VMEM((HEADS, NX, NY, 1, 128), f32),
            pltpu.VMEM((HEADS, NX - 1, NY, 16, DH), bf16),
            pltpu.VMEM((HEADS, NY - 1, NX, 16, DH), bf16),
            pltpu.VMEM((HEADS, NX - 1, NY, 1, 128), f32),
            pltpu.VMEM((HEADS, NY - 1, NX, 1, 128), f32),
            pltpu.VMEM((HEADS, NY, 16, DH), bf16),
            pltpu.VMEM((HEADS, NX, 16, DH), bf16),
            pltpu.VMEM((HEADS, NY, 1, 128), f32),
            pltpu.VMEM((HEADS, NX, 1, 128), f32),
            pltpu.VMEM((HEADS, NY - 1, 16, DH), bf16),
            pltpu.VMEM((HEADS, NX - 1, 16, DH), bf16),
            pltpu.VMEM((HEADS, NY - 1, 1, 128), f32),
            pltpu.VMEM((HEADS, NX - 1, 1, 128), f32),
            pltpu.VMEM((HEADS, 16, WIDE), bf16),
            pltpu.VMEM((HEADS, 1, 128), f32),
            pltpu.VMEM((NZ - 1, 16, WIDE), bf16),
            pltpu.VMEM((NZ - 1, 1, 128), f32),
            pltpu.VMEM((4 * HEADS, 16, DH), bf16),
            dma((3,)), heads, heads, dma,
            heads, heads, heads, heads, heads, heads,
            heads, heads, heads, heads, heads, heads, heads, heads,
            heads, heads, heads, heads, heads, heads, heads, heads,
            dma((HEADS, 2)), dma, dma((HEADS, 2)), dma, dma((4,)), dma,
            pltpu.SemaphoreType.REGULAR((3,)),
        ],
        compiler_params=pltpu.CompilerParams(
            collective_id=0, has_side_effects=True, vmem_limit_bytes=64 * 1024 * 1024
        ),
        cost_estimate=pl.CostEstimate(flops=800_000_000, bytes_accessed=8_000_000, transcendentals=1_000_000),
    )(offset, lambdas, gain, queries, keys, values)


def solution(mesh):
    return jax.shard_map(
        per_device,
        mesh=mesh,
        in_specs=(P("blk", None), P(("ctx", "blk"), None), P(("ctx", "blk"), None), P(), P(), P()),
        out_specs=P("blk", None),
        check_vma=False,
    )
```

```python
import functools
import math

import jax
import jax.numpy as jnp
from jax import lax
from jax.experimental import pallas as pl
from jax.experimental.pallas import tpu as pltpu
from jax.sharding import PartitionSpec as P

NX, NY, NZ = 4, 4, 16
CHUNK = 8
HEADS = 5
HALF_Z = NZ // 2
REACH = 3
DH = 128
WIDE = 2 * DH
KEYS = 384
HIDDEN = -1e30
MESH = pl.DeviceIdType.MESH


LAG = 2


def wrap(index, size):
    return jnp.where(index >= size, index - size, index)


def wait_bytes(ref, sem):
    pltpu.make_async_copy(ref, ref, sem).wait()


def send(src, dst, ssem, rsem, to):
    copy = pltpu.make_async_remote_copy(
        src_ref=src, dst_ref=dst, send_sem=ssem, recv_sem=rsem, device_id=to, device_id_type=MESH
    )
    copy.start()
    return copy


def loop(count, body, start=0):
    def step(i, carry):
        body(i)
        return carry

    lax.fori_loop(start, count, step, 0)


def merge_rows(rows):
    top = functools.reduce(jnp.maximum, rows)
    parts = [jnp.exp2(row - top) for row in rows]
    total = functools.reduce(jnp.add, parts)
    inverse = 1.0 / total
    return [part * inverse for part in parts], top + jnp.log2(total)


def column(row):
    lead = row.shape[:-2]
    lane = lax.broadcasted_iota(jnp.int32, lead + (16, 128), len(lead) + 1)
    sub = lax.broadcasted_iota(jnp.int32, lead + (16, 128), len(lead))
    wide = jnp.where(lane == sub, jnp.broadcast_to(row, lead + (16, 128)), 0.0)
    return jnp.sum(wide, axis=-1, keepdims=True)


def weighted(weights, parts):
    acc = None
    for weight, part in zip(weights, parts):
        term = column(weight) * part.astype(jnp.float32)
        acc = term if acc is None else acc + term
    return acc


def kernel(
    offset_hbm, lam_hbm, gain_hbm, q_ref, k_ref, v_ref, out_ref,
    offset_ref, lam_ref, gain_ref,
    kbuf, vbuf, qbuf, bias, tall, scores, expo, inverse, maps, obuf, sbuf, part, part_row,
    zsend, zsrow, zbuf, zsbuf, fin,
    small_sem, kl_sem, vl_sem, ql_sem, k_ssem, k_rsem, v_ssem, v_rsem, q_ssem, q_rsem,
    p_ssem, p_rsem, pr_ssem, pr_rsem,
    z_ssem, z_rsem, zt_ssem, zt_rsem, g_ssem, g_rsem, token_sem,
):
    ctx = lax.axis_index("ctx")
    blk = lax.axis_index("blk")
    core = lax.rem(ctx, 2)
    z = lax.rem(ctx // 2, NZ)
    y_lo = ctx // (2 * NZ)
    x = blk // 2
    y = lax.rem(blk, 2) * 2 + y_lo
    other = 1 - core
    y_hi = lax.rem(blk, 2)
    xs = [wrap(x + d, NX) for d in range(1, NX)]
    ys = [wrap(y + d, NY) for d in range(1, NY)]
    beside = (ctx + other - core, blk)
    pair = (ctx + 2 * NZ * (1 - 2 * y_lo), blk)
    ctx_of = [(lax.rem(yy, 2) * NZ + z) * 2 + core for yy in [y] + ys]
    hi_of = [yy // 2 for yy in [y] + ys]
    plane = [
        (xx, yy, (ctx_of[j], xx * 2 + hi_of[j]))
        for xx in [x] + xs
        for j, yy in enumerate([y] + ys)
    ][1:]
    x_line = [(ctx, xx * 2 + y_hi) for xx in xs]
    mirror = [(pair[0], xx * 2 + 1 - y_hi) for xx in [x] + xs]
    z_base = y_lo * 2 * NZ + core

    def z_line(d):
        return (z_base + 2 * wrap(z + d, NZ), blk)

    steps = (0, other - core, 2 * NZ * (1 - 2 * y_lo), 2 * NZ * (1 - 2 * y_lo) + other - core)

    def column_at(i, zz):
        return (z_base + steps[i] + 2 * zz, blk)

    def cols(which, head, count=1):
        return pl.ds(pl.multiple_of(which * (HEADS * WIDE) + head * WIDE, WIDE), count * WIDE)

    barrier = pltpu.get_barrier_semaphore()

    def greet(to):
        pl.semaphore_signal(barrier, inc=1, device_id=to, device_id_type=MESH)

    near = [beside] + [to for _, _, to in plane] + [z_line(1), z_line(NZ - 1), column_at(3, z)]
    for to in near:
        greet(to)

    def own_copies(h):
        return (
            pltpu.make_async_copy(k_ref.at[:, cols(core, h)], kbuf.at[h, pl.ds(0, KEYS)], kl_sem.at[h]),
            pltpu.make_async_copy(v_ref.at[:, cols(core, h)], vbuf.at[h, pl.ds(0, KEYS)], vl_sem.at[h]),
        )

    def start_own(h):
        for copy in own_copies(h):
            copy.start()

    own_q = pltpu.make_async_copy(q_ref.at[:, cols(core, 0, HEADS)], qbuf.at[blk], ql_sem)
    own_q.start()
    loop(HEADS, start_own)
    small = [
        pltpu.make_async_copy(offset_hbm, offset_ref, small_sem.at[0]),
        pltpu.make_async_copy(lam_hbm, lam_ref, small_sem.at[1]),
        pltpu.make_async_copy(gain_hbm, gain_ref, small_sem.at[2]),
    ]
    for copy in small:
        copy.start()
    pl.semaphore_wait(barrier, len(near))

    def pushes(h):
        return (
            pltpu.make_async_remote_copy(
                src_ref=k_ref.at[:, cols(other, h)], dst_ref=kbuf.at[h, pl.ds(KEYS, KEYS)], send_sem=k_ssem.at[h],
                recv_sem=k_rsem.at[h], device_id=beside, device_id_type=MESH,
            ),
            pltpu.make_async_remote_copy(
                src_ref=v_ref.at[:, cols(other, h)], dst_ref=vbuf.at[h, pl.ds(KEYS, KEYS)], send_sem=v_ssem.at[h],
                recv_sem=v_rsem.at[h], device_id=beside, device_id_type=MESH,
            ),
        )

    def push(h):
        for copy in pushes(h):
            copy.start()

    def queries_of(h):
        return qbuf.at[pl.ds(0, 7), :, cols(0, h)]

    def push_head(h):
        mine = q_ref.at[:, cols(core, h)]
        for to in mirror + x_line:
            send(mine, qbuf.at[blk, :, cols(0, h)], q_ssem.at[h], q_rsem.at[h], to)
        push(h)

    loop(HEADS, push_head)

    def token(step):
        for d in (2**step, NZ - 2**step):
            pl.semaphore_signal(token_sem.at[step], inc=1, device_id=z_line(d), device_id_type=MESH)

    token(0)

    row = lax.broadcasted_iota(jnp.int32, (32 * CHUNK, KEYS), 0)
    pos = lax.broadcasted_iota(jnp.int32, (32 * CHUNK, KEYS), 1)
    ahead = pos - (lax.shift_right_logical(row, 4) * CHUNK + (row & (CHUNK - 1)))
    small[0].wait()
    for s in range(2):
        owner = ctx if s == 0 else ctx + other - core
        start = (owner * 8 + blk) * KEYS
        bias[:, s * KEYS : s * KEYS + KEYS] = jnp.where(ahead <= offset_ref[0] - start, 0.0, HIDDEN)

    scale = DH ** (-0.5) * math.log2(math.e)

    def attend(h):
        own_k, own_v = own_copies(h)
        wait_bytes(queries_of(h), q_rsem.at[h])
        blocks = [slice(32 * b, 32 * b + 32) for b in range(8)]
        lane = lax.broadcasted_iota(jnp.int32, (2, CHUNK, WIDE), 2)
        for b, rows in enumerate(blocks):
            q = qbuf[b, :, cols(0, h)].astype(jnp.float32).reshape(2, CHUNK, WIDE)
            both = jnp.concatenate([jnp.where(lane < DH, q, 0.0), jnp.where(lane >= DH, q, 0.0)], axis=1)
            tall[rows] = both.reshape(32, WIDE).astype(jnp.bfloat16)
        own_k.wait()
        wait_bytes(kbuf.at[h, pl.ds(KEYS, KEYS)], k_rsem.at[h])
        scores[...] = lax.dot_general(
            tall[...], kbuf[h], (((1,), (1,)), ((), ())), preferred_element_type=jnp.float32
        )
        stat_lane = lax.broadcasted_iota(jnp.int32, (2, 16, 128), 2)
        stat_sub = lax.broadcasted_iota(jnp.int32, (2, 16, 128), 1)
        for b, rows in enumerate(blocks):
            score = scores[rows] * scale + bias[rows]
            top = jnp.max(score, axis=1, keepdims=True)
            e = jnp.exp2(score - top)
            total = jnp.sum(e, axis=1, keepdims=True)
            expo[rows] = e.astype(jnp.bfloat16)
            inverse[rows] = jnp.broadcast_to(1.0 / total, (32, 128))
            stat = jnp.broadcast_to((top + jnp.log2(total)).reshape(2, 16, 1), (2, 16, 128))
            stat = jnp.where(stat_lane == stat_sub, stat, 0.0)
            sbuf[h, b // 2, (b % 2) * 2 : (b % 2) * 2 + 2] = jnp.sum(stat, axis=1, keepdims=True)
        own_v.wait()
        wait_bytes(vbuf.at[h, pl.ds(KEYS, KEYS)], v_rsem.at[h])
        maps[...] = jnp.dot(expo[...], vbuf[h], preferred_element_type=jnp.float32)
        for b, rows in enumerate(blocks):
            for half in range(2):
                lanes = slice(half * DH, half * DH + DH)
                out = (maps[rows, lanes] * inverse[rows]).reshape(2, 16, DH).astype(jnp.bfloat16)
                obuf[h, b // 2, (b % 2) * 2 : (b % 2) * 2 + 2, :, lanes] = out
        for d, (xx, yy, to) in enumerate(plane):
            send(sbuf.at[h, xx, yy], part_row.at[h, d], pr_ssem.at[h], pr_rsem.at[h], to)
            send(obuf.at[h, xx, yy], part.at[h, d], p_ssem.at[h], p_rsem.at[h], to)

    def owner_of(h):
        return lax.rem(3 * h + HALF_Z - core, HALF_Z)

    def reduce(h):
        count = NX * NY - 1
        wait_bytes(part_row.at[h], pr_rsem.at[h])
        weights, whole = merge_rows([sbuf[h, x, y]] + [part_row[h, d] for d in range(count)])
        zsrow[h] = whole
        wait_bytes(part.at[h], p_rsem.at[h])
        merged = weighted(weights, [obuf[h, x, y]] + [part[h, d] for d in range(count)])
        zsend[h] = merged.astype(jnp.bfloat16)
        for i in range(2):
            owner = owner_of(h) + i * HALF_Z
            gap = wrap(owner - z + NZ, NZ)

            @pl.when(gap != 0)
            def _():
                to = (z_base + 2 * owner, blk)
                send(zsrow.at[h], zsbuf.at[gap - 1], zt_ssem.at[h, i], zt_rsem, to)
                send(zsend.at[h], zbuf.at[gap - 1], z_ssem.at[h, i], z_rsem, to)

    def turn_of(i):
        @pl.when(i < HEADS)
        def _():
            attend(i)

        @pl.when(i == 0)
        def _():
            pl.semaphore_wait(token_sem.at[1], 2)
            token(2)

        @pl.when(i == LAG)
        def _():
            pl.semaphore_wait(token_sem.at[2], 2)

        @pl.when(i >= LAG)
        def _():
            reduce(i - LAG)

    own_q.wait()
    pl.semaphore_wait(token_sem.at[0], 2)
    token(1)
    loop(HEADS + LAG, turn_of)

    mine = lax.rem(3 * (z + core), HALF_Z)
    is_owner = mine < HEADS
    all_tiles = 4 * HEADS
    small[1].wait()
    small[2].wait()

    @pl.when(is_owner)
    def _():
        wait_bytes(zsbuf, zt_rsem)
        weights, _ = merge_rows([zsrow[mine]] + [zsbuf[d] for d in range(NZ - 1)])
        wait_bytes(zbuf, z_rsem)
        acc = weighted(weights, [zsend[mine]] + [zbuf[d] for d in range(NZ - 1)])
        head = core * HEADS + mine
        attended = acc[:CHUNK] - lam_ref[head] * acc[CHUNK:]
        spread = jnp.sqrt(jnp.mean(attended * attended, axis=-1, keepdims=True) + 1e-5)
        normed = attended / spread * gain_ref[cols(0, head)].reshape(1, WIDE)
        halves = jnp.concatenate([normed[:, :DH], normed[:, DH:]], axis=0)
        slot = (y_lo * 2 + core) * HEADS + mine
        fin[slot] = halves.astype(jnp.bfloat16)
        tile = fin.at[slot]

        def give(d):
            zz = wrap(wrap(z + d + NZ - REACH, 2 * NZ), NZ)
            for i in range(1, 4):
                send(tile, tile, g_ssem.at[i], g_rsem, column_at(i, zz))

            @pl.when(zz != z)
            def _():
                send(tile, tile, g_ssem.at[0], g_rsem, column_at(0, zz))

        loop(HALF_Z, give)
        wait_bytes(fin.at[pl.ds(0, all_tiles - 1)], g_rsem)

    @pl.when(jnp.logical_not(is_owner))
    def _():
        wait_bytes(fin, g_rsem)

    def assemble(h):
        for c in range(2):
            first = fin[c * HEADS + h].astype(jnp.float32)
            second = fin[(2 + c) * HEADS + h].astype(jnp.float32)
            low = jnp.concatenate([first[:CHUNK], second[:CHUNK]], axis=0)
            high = jnp.concatenate([first[CHUNK:], second[CHUNK:]], axis=0)
            out_ref[:, cols(c, h)] = jnp.concatenate([low, high], axis=1).astype(jnp.bfloat16)

    loop(HEADS, assemble)

    def left(h):
        for copy in pushes(h):
            copy.wait_send()
        wait_bytes(queries_of(h), q_ssem.at[h])
        wait_bytes(part.at[h], p_ssem.at[h])
        wait_bytes(part_row.at[h], pr_ssem.at[h])

        for i in range(2):

            @pl.when(owner_of(h) + i * HALF_Z != z)
            def _():
                wait_bytes(zsend.at[h], z_ssem.at[h, i])
                wait_bytes(zsrow.at[h], zt_ssem.at[h, i])

    loop(HEADS, left)
    @pl.when(is_owner)
    def _():
        wait_bytes(fin.at[pl.ds(0, HALF_Z - 1)], g_ssem.at[0])
        for i in range(1, 4):
            wait_bytes(fin.at[pl.ds(0, HALF_Z)], g_ssem.at[i])


def per_device(queries, keys, values, offset, lambdas, gain):
    row_count, width = queries.shape
    bf16, f32 = jnp.bfloat16, jnp.float32
    dma = pltpu.SemaphoreType.DMA
    heads = dma((HEADS,))
    hbm = pl.BlockSpec(memory_space=pltpu.HBM)
    vmem = pl.BlockSpec(memory_space=pltpu.VMEM)
    return pl.pallas_call(
        kernel,
        out_shape=jax.ShapeDtypeStruct((row_count, width), bf16),
        in_specs=[hbm] * 6,
        out_specs=vmem,
        scratch_shapes=[
            pltpu.SMEM((1,), jnp.int32),
            pltpu.SMEM(lambdas.shape, f32),
            pltpu.VMEM(gain.shape, f32),
            pltpu.VMEM((HEADS, 2 * KEYS, WIDE), bf16),
            pltpu.VMEM((HEADS, 2 * KEYS, WIDE), bf16),
            pltpu.VMEM((8, 16, HEADS * WIDE), bf16),
            pltpu.VMEM((256, 2 * KEYS), f32),
            pltpu.VMEM((256, WIDE), bf16),
            pltpu.VMEM((256, 2 * KEYS), f32),
            pltpu.VMEM((256, 2 * KEYS), bf16),
            pltpu.VMEM((256, 128), f32),
            pltpu.VMEM((256, WIDE), f32),
            pltpu.VMEM((HEADS, NX, NY, 16, WIDE), bf16),
            pltpu.VMEM((HEADS, NX, NY, 1, 128), f32),
            pltpu.VMEM((HEADS, NX * NY - 1, 16, WIDE), bf16),
            pltpu.VMEM((HEADS, NX * NY - 1, 1, 128), f32),
            pltpu.VMEM((HEADS, 16, WIDE), bf16),
            pltpu.VMEM((HEADS, 1, 128), f32),
            pltpu.VMEM((NZ - 1, 16, WIDE), bf16),
            pltpu.VMEM((NZ - 1, 1, 128), f32),
            pltpu.VMEM((4 * HEADS, 16, DH), bf16),
            dma((3,)), heads, heads, dma,
            heads, heads, heads, heads, heads, heads,
            heads, heads, heads, heads,
            dma((HEADS, 2)), dma, dma((HEADS, 2)), dma, dma((4,)), dma,
            pltpu.SemaphoreType.REGULAR((3,)),
        ],
        compiler_params=pltpu.CompilerParams(
            collective_id=0, has_side_effects=True, vmem_limit_bytes=64 * 1024 * 1024
        ),
        cost_estimate=pl.CostEstimate(flops=800_000_000, bytes_accessed=8_000_000, transcendentals=1_000_000),
    )(offset, lambdas, gain, queries, keys, values)


def solution(mesh):
    return jax.shard_map(
        per_device,
        mesh=mesh,
        in_specs=(P("blk", None), P(("ctx", "blk"), None), P(("ctx", "blk"), None), P(), P(), P()),
        out_specs=P("blk", None),
        check_vma=False,
    )
```

```python
import functools
import math

import jax
import jax.numpy as jnp
from jax import lax
from jax.experimental import pallas as pl
from jax.experimental.pallas import tpu as pltpu
from jax.sharding import PartitionSpec as P

NX, NY, NZ = 4, 4, 16
CHUNK = 8
HEADS = 5
HALF_Z = NZ // 2
REACH = 3
DH = 128
WIDE = 2 * DH
KEYS = 384
HIDDEN = -1e30
MESH = pl.DeviceIdType.MESH


LAG = 2


def wrap(index, size):
    return jnp.where(index >= size, index - size, index)


def wait_bytes(ref, sem):
    pltpu.make_async_copy(ref, ref, sem).wait()


def send(src, dst, ssem, rsem, to):
    copy = pltpu.make_async_remote_copy(
        src_ref=src, dst_ref=dst, send_sem=ssem, recv_sem=rsem, device_id=to, device_id_type=MESH
    )
    copy.start()
    return copy


def loop(count, body, start=0):
    def step(i, carry):
        body(i)
        return carry

    lax.fori_loop(start, count, step, 0)


def merge_rows(rows):
    top = functools.reduce(jnp.maximum, rows)
    parts = [jnp.exp2(row - top) for row in rows]
    total = functools.reduce(jnp.add, parts)
    inverse = 1.0 / total
    return [part * inverse for part in parts], top + jnp.log2(total)


def column(row):
    lead = row.shape[:-2]
    lane = lax.broadcasted_iota(jnp.int32, lead + (16, 128), len(lead) + 1)
    sub = lax.broadcasted_iota(jnp.int32, lead + (16, 128), len(lead))
    wide = jnp.where(lane == sub, jnp.broadcast_to(row, lead + (16, 128)), 0.0)
    return jnp.sum(wide, axis=-1, keepdims=True)


def weighted(weights, parts):
    acc = None
    for weight, part in zip(weights, parts):
        term = column(weight) * part.astype(jnp.float32)
        acc = term if acc is None else acc + term
    return acc


def kernel(
    offset_hbm, lam_hbm, gain_hbm, q_ref, k_ref, v_ref, out_ref,
    offset_ref, lam_ref, gain_ref,
    kbuf, vbuf, qbuf, bias, tall, scores, expo, inverse, maps, obuf, sbuf, part, part_row,
    zsend, zsrow, zbuf, zsbuf, fin,
    small_sem, kl_sem, vl_sem, ql_sem, k_ssem, k_rsem, v_ssem, v_rsem, q_ssem, q_rsem,
    p_ssem, p_rsem, pr_ssem, pr_rsem,
    z_ssem, z_rsem, zt_ssem, zt_rsem, g_ssem, g_rsem, token_sem,
):
    ctx = lax.axis_index("ctx")
    blk = lax.axis_index("blk")
    core = lax.rem(ctx, 2)
    z = lax.rem(ctx // 2, NZ)
    y_lo = ctx // (2 * NZ)
    x = blk // 2
    y = lax.rem(blk, 2) * 2 + y_lo
    other = 1 - core
    y_hi = lax.rem(blk, 2)
    xs = [wrap(x + d, NX) for d in range(1, NX)]
    ys = [wrap(y + d, NY) for d in range(1, NY)]
    beside = (ctx + other - core, blk)
    pair = (ctx + 2 * NZ * (1 - 2 * y_lo), blk)
    ctx_of = [(lax.rem(yy, 2) * NZ + z) * 2 + core for yy in [y] + ys]
    hi_of = [yy // 2 for yy in [y] + ys]
    plane = [
        (xx, yy, (ctx_of[j], xx * 2 + hi_of[j]))
        for xx in [x] + xs
        for j, yy in enumerate([y] + ys)
    ][1:]
    x_line = [(ctx, xx * 2 + y_hi) for xx in xs]
    mirror = [(pair[0], xx * 2 + 1 - y_hi) for xx in [x] + xs]
    z_base = y_lo * 2 * NZ + core

    def z_line(d):
        return (z_base + 2 * wrap(z + d, NZ), blk)

    steps = (0, other - core, 2 * NZ * (1 - 2 * y_lo), 2 * NZ * (1 - 2 * y_lo) + other - core)

    def column_at(i, zz):
        return (z_base + steps[i] + 2 * zz, blk)

    def cols(which, head, count=1):
        return pl.ds(pl.multiple_of(which * (HEADS * WIDE) + head * WIDE, WIDE), count * WIDE)

    barrier = pltpu.get_barrier_semaphore()

    def greet(to):
        pl.semaphore_signal(barrier, inc=1, device_id=to, device_id_type=MESH)

    near = [beside] + [to for _, _, to in plane] + [z_line(1), z_line(NZ - 1), column_at(3, z)]
    for to in near:
        greet(to)

    def own_copies(h):
        return (
            pltpu.make_async_copy(k_ref.at[:, cols(core, h)], kbuf.at[h, pl.ds(0, KEYS)], kl_sem.at[h]),
            pltpu.make_async_copy(v_ref.at[:, cols(core, h)], vbuf.at[h, pl.ds(0, KEYS)], vl_sem.at[h]),
        )

    def start_own(h):
        for copy in own_copies(h):
            copy.start()

    own_q = pltpu.make_async_copy(q_ref.at[:, cols(core, 0, HEADS)], qbuf.at[blk], ql_sem)
    own_q.start()
    loop(HEADS, start_own)
    small = [
        pltpu.make_async_copy(offset_hbm, offset_ref, small_sem.at[0]),
        pltpu.make_async_copy(lam_hbm, lam_ref, small_sem.at[1]),
        pltpu.make_async_copy(gain_hbm, gain_ref, small_sem.at[2]),
    ]
    for copy in small:
        copy.start()
    pl.semaphore_wait(barrier, len(near))

    def pushes(h):
        return (
            pltpu.make_async_remote_copy(
                src_ref=k_ref.at[:, cols(other, h)], dst_ref=kbuf.at[h, pl.ds(KEYS, KEYS)], send_sem=k_ssem.at[h],
                recv_sem=k_rsem.at[h], device_id=beside, device_id_type=MESH,
            ),
            pltpu.make_async_remote_copy(
                src_ref=v_ref.at[:, cols(other, h)], dst_ref=vbuf.at[h, pl.ds(KEYS, KEYS)], send_sem=v_ssem.at[h],
                recv_sem=v_rsem.at[h], device_id=beside, device_id_type=MESH,
            ),
        )

    def push(h):
        for copy in pushes(h):
            copy.start()

    def queries_of(h):
        return qbuf.at[pl.ds(0, 7), :, cols(0, h)]

    def push_head(h):
        mine = q_ref.at[:, cols(core, h)]
        for to in mirror + x_line:
            send(mine, qbuf.at[blk, :, cols(0, h)], q_ssem.at[h], q_rsem.at[h], to)
        push(h)

    loop(HEADS, push_head)

    def token(step):
        for d in (2**step, NZ - 2**step):
            pl.semaphore_signal(token_sem.at[step], inc=1, device_id=z_line(d), device_id_type=MESH)

    token(0)

    row = lax.broadcasted_iota(jnp.int32, (32 * CHUNK, KEYS), 0)
    pos = lax.broadcasted_iota(jnp.int32, (32 * CHUNK, KEYS), 1)
    ahead = pos - (lax.shift_right_logical(row, 4) * CHUNK + (row & (CHUNK - 1)))
    small[0].wait()
    for s in range(2):
        owner = ctx if s == 0 else ctx + other - core
        start = (owner * 8 + blk) * KEYS
        bias[:, s * KEYS : s * KEYS + KEYS] = jnp.where(ahead <= offset_ref[0] - start, 0.0, HIDDEN)

    scale = DH ** (-0.5) * math.log2(math.e)

    blocks = [slice(32 * b, 32 * b + 32) for b in range(8)]

    def prepare(h):
        wait_bytes(queries_of(h), q_rsem.at[h])
        lane = lax.broadcasted_iota(jnp.int32, (2, CHUNK, WIDE), 2)
        for b, rows in enumerate(blocks):
            q = qbuf[b, :, cols(0, h)].astype(jnp.float32).reshape(2, CHUNK, WIDE)
            both = jnp.concatenate([jnp.where(lane < DH, q, 0.0), jnp.where(lane >= DH, q, 0.0)], axis=1)
            tall[h % 2, rows] = both.reshape(32, WIDE).astype(jnp.bfloat16)
        own_copies(h)[0].wait()
        wait_bytes(kbuf.at[h, pl.ds(KEYS, KEYS)], k_rsem.at[h])

    def score(h, tile):
        keys = slice(256 * tile, 256 * tile + 256)
        scores[h % 2, :, keys] = lax.dot_general(
            tall[h % 2], kbuf[h, keys], (((1,), (1,)), ((), ())), preferred_element_type=jnp.float32
        )

    stat_lane = lax.broadcasted_iota(jnp.int32, (2, 16, 128), 2)
    stat_sub = lax.broadcasted_iota(jnp.int32, (2, 16, 128), 1)

    def soften(h, b):
        rows = blocks[b]
        values = scores[h % 2, rows] * scale + bias[rows]
        top = jnp.max(values, axis=1, keepdims=True)
        e = jnp.exp2(values - top)
        total = jnp.sum(e, axis=1, keepdims=True)
        expo[rows] = e.astype(jnp.bfloat16)
        inverse[rows] = jnp.broadcast_to(1.0 / total, (32, 128))
        stat = jnp.broadcast_to((top + jnp.log2(total)).reshape(2, 16, 1), (2, 16, 128))
        stat = jnp.where(stat_lane == stat_sub, stat, 0.0)
        sbuf[h, b // 2, (b % 2) * 2 : (b % 2) * 2 + 2] = jnp.sum(stat, axis=1, keepdims=True)

    def attend(h):
        own_v = own_copies(h)[1]
        if h + 1 < HEADS:
            prepare(h + 1)
        for tile, some in enumerate(((0, 1, 2), (3, 4, 5), (6, 7))):
            if h + 1 < HEADS:
                score(h + 1, tile)
            for b in some:
                soften(h, b)
        own_v.wait()
        wait_bytes(vbuf.at[h, pl.ds(KEYS, KEYS)], v_rsem.at[h])
        maps[...] = jnp.dot(expo[...], vbuf[h], preferred_element_type=jnp.float32)
        for b, rows in enumerate(blocks):
            for half in range(2):
                lanes = slice(half * DH, half * DH + DH)
                out = (maps[rows, lanes] * inverse[rows]).reshape(2, 16, DH).astype(jnp.bfloat16)
                obuf[h, b // 2, (b % 2) * 2 : (b % 2) * 2 + 2, :, lanes] = out
        for d, (xx, yy, to) in enumerate(plane):
            send(sbuf.at[h, xx, yy], part_row.at[h, d], pr_ssem.at[h], pr_rsem.at[h], to)
            send(obuf.at[h, xx, yy], part.at[h, d], p_ssem.at[h], p_rsem.at[h], to)

    def owner_of(h):
        return lax.rem(3 * h + HALF_Z - core, HALF_Z)

    def reduce(h):
        count = NX * NY - 1
        wait_bytes(part_row.at[h], pr_rsem.at[h])
        weights, whole = merge_rows([sbuf[h, x, y]] + [part_row[h, d] for d in range(count)])
        zsrow[h] = whole
        wait_bytes(part.at[h], p_rsem.at[h])
        merged = weighted(weights, [obuf[h, x, y]] + [part[h, d] for d in range(count)])
        zsend[h] = merged.astype(jnp.bfloat16)
        for i in range(2):
            owner = owner_of(h) + i * HALF_Z
            gap = wrap(owner - z + NZ, NZ)

            @pl.when(gap != 0)
            def _():
                to = (z_base + 2 * owner, blk)
                send(zsrow.at[h], zsbuf.at[gap - 1], zt_ssem.at[h, i], zt_rsem, to)
                send(zsend.at[h], zbuf.at[gap - 1], z_ssem.at[h, i], z_rsem, to)

    own_q.wait()
    pl.semaphore_wait(token_sem.at[0], 2)
    token(1)
    prepare(0)
    for tile in range(3):
        score(0, tile)
    for i in range(HEADS + LAG):
        if i < HEADS:
            attend(i)
        if i == 0:
            pl.semaphore_wait(token_sem.at[1], 2)
            token(2)
        if i == LAG:
            pl.semaphore_wait(token_sem.at[2], 2)
        if i >= LAG:
            reduce(i - LAG)

    mine = lax.rem(3 * (z + core), HALF_Z)
    is_owner = mine < HEADS
    all_tiles = 4 * HEADS
    small[1].wait()
    small[2].wait()

    @pl.when(is_owner)
    def _():
        wait_bytes(zsbuf, zt_rsem)
        weights, _ = merge_rows([zsrow[mine]] + [zsbuf[d] for d in range(NZ - 1)])
        wait_bytes(zbuf, z_rsem)
        acc = weighted(weights, [zsend[mine]] + [zbuf[d] for d in range(NZ - 1)])
        head = core * HEADS + mine
        attended = acc[:CHUNK] - lam_ref[head] * acc[CHUNK:]
        spread = jnp.sqrt(jnp.mean(attended * attended, axis=-1, keepdims=True) + 1e-5)
        normed = attended / spread * gain_ref[cols(0, head)].reshape(1, WIDE)
        halves = jnp.concatenate([normed[:, :DH], normed[:, DH:]], axis=0)
        slot = (y_lo * 2 + core) * HEADS + mine
        fin[slot] = halves.astype(jnp.bfloat16)
        tile = fin.at[slot]

        def give(d):
            zz = wrap(wrap(z + d + NZ - REACH, 2 * NZ), NZ)
            for i in range(1, 4):
                send(tile, tile, g_ssem.at[i], g_rsem, column_at(i, zz))

            @pl.when(zz != z)
            def _():
                send(tile, tile, g_ssem.at[0], g_rsem, column_at(0, zz))

        loop(HALF_Z, give)
        wait_bytes(fin.at[pl.ds(0, all_tiles - 1)], g_rsem)

    @pl.when(jnp.logical_not(is_owner))
    def _():
        wait_bytes(fin, g_rsem)

    def assemble(h):
        for c in range(2):
            first = fin[c * HEADS + h].astype(jnp.float32)
            second = fin[(2 + c) * HEADS + h].astype(jnp.float32)
            low = jnp.concatenate([first[:CHUNK], second[:CHUNK]], axis=0)
            high = jnp.concatenate([first[CHUNK:], second[CHUNK:]], axis=0)
            out_ref[:, cols(c, h)] = jnp.concatenate([low, high], axis=1).astype(jnp.bfloat16)

    loop(HEADS, assemble)

    def left(h):
        for copy in pushes(h):
            copy.wait_send()
        wait_bytes(queries_of(h), q_ssem.at[h])
        wait_bytes(part.at[h], p_ssem.at[h])
        wait_bytes(part_row.at[h], pr_ssem.at[h])

        for i in range(2):

            @pl.when(owner_of(h) + i * HALF_Z != z)
            def _():
                wait_bytes(zsend.at[h], z_ssem.at[h, i])
                wait_bytes(zsrow.at[h], zt_ssem.at[h, i])

    loop(HEADS, left)
    @pl.when(is_owner)
    def _():
        wait_bytes(fin.at[pl.ds(0, HALF_Z - 1)], g_ssem.at[0])
        for i in range(1, 4):
            wait_bytes(fin.at[pl.ds(0, HALF_Z)], g_ssem.at[i])


def per_device(queries, keys, values, offset, lambdas, gain):
    row_count, width = queries.shape
    bf16, f32 = jnp.bfloat16, jnp.float32
    dma = pltpu.SemaphoreType.DMA
    heads = dma((HEADS,))
    hbm = pl.BlockSpec(memory_space=pltpu.HBM)
    vmem = pl.BlockSpec(memory_space=pltpu.VMEM)
    return pl.pallas_call(
        kernel,
        out_shape=jax.ShapeDtypeStruct((row_count, width), bf16),
        in_specs=[hbm] * 6,
        out_specs=vmem,
        scratch_shapes=[
            pltpu.SMEM((1,), jnp.int32),
            pltpu.SMEM(lambdas.shape, f32),
            pltpu.VMEM(gain.shape, f32),
            pltpu.VMEM((HEADS, 2 * KEYS, WIDE), bf16),
            pltpu.VMEM((HEADS, 2 * KEYS, WIDE), bf16),
            pltpu.VMEM((8, 16, HEADS * WIDE), bf16),
            pltpu.VMEM((256, 2 * KEYS), f32),
            pltpu.VMEM((2, 256, WIDE), bf16),
            pltpu.VMEM((2, 256, 2 * KEYS), f32),
            pltpu.VMEM((256, 2 * KEYS), bf16),
            pltpu.VMEM((256, 128), f32),
            pltpu.VMEM((256, WIDE), f32),
            pltpu.VMEM((HEADS, NX, NY, 16, WIDE), bf16),
            pltpu.VMEM((HEADS, NX, NY, 1, 128), f32),
            pltpu.VMEM((HEADS, NX * NY - 1, 16, WIDE), bf16),
            pltpu.VMEM((HEADS, NX * NY - 1, 1, 128), f32),
            pltpu.VMEM((HEADS, 16, WIDE), bf16),
            pltpu.VMEM((HEADS, 1, 128), f32),
            pltpu.VMEM((NZ - 1, 16, WIDE), bf16),
            pltpu.VMEM((NZ - 1, 1, 128), f32),
            pltpu.VMEM((4 * HEADS, 16, DH), bf16),
            dma((3,)), heads, heads, dma,
            heads, heads, heads, heads, heads, heads,
            heads, heads, heads, heads,
            dma((HEADS, 2)), dma, dma((HEADS, 2)), dma, dma((4,)), dma,
            pltpu.SemaphoreType.REGULAR((3,)),
        ],
        compiler_params=pltpu.CompilerParams(
            collective_id=0, has_side_effects=True, vmem_limit_bytes=64 * 1024 * 1024
        ),
        cost_estimate=pl.CostEstimate(flops=800_000_000, bytes_accessed=8_000_000, transcendentals=1_000_000),
    )(offset, lambdas, gain, queries, keys, values)


def solution(mesh):
    return jax.shard_map(
        per_device,
        mesh=mesh,
        in_specs=(P("blk", None), P(("ctx", "blk"), None), P(("ctx", "blk"), None), P(), P(), P()),
        out_specs=P("blk", None),
        check_vma=False,
    )
```

```python
import functools
import math

import jax
import jax.numpy as jnp
from jax import lax
from jax.experimental import pallas as pl
from jax.experimental.pallas import tpu as pltpu
from jax.sharding import PartitionSpec as P

NX, NY, NZ = 4, 4, 16
CHUNK = 8
HEADS = 5
HALF_Z = NZ // 2
REACH = 3
DH = 128
WIDE = 2 * DH
KEYS = 384
HIDDEN = -1e30
MESH = pl.DeviceIdType.MESH


LAG = 2
TWO = 3


def wrap(index, size):
    return jnp.where(index >= size, index - size, index)


def wait_bytes(ref, sem):
    pltpu.make_async_copy(ref, ref, sem).wait()


def send(src, dst, ssem, rsem, to):
    copy = pltpu.make_async_remote_copy(
        src_ref=src, dst_ref=dst, send_sem=ssem, recv_sem=rsem, device_id=to, device_id_type=MESH
    )
    copy.start()
    return copy


def loop(count, body, start=0):
    def step(i, carry):
        body(i)
        return carry

    lax.fori_loop(start, count, step, 0)


def merge_rows(rows):
    top = functools.reduce(jnp.maximum, rows)
    parts = [jnp.exp2(row - top) for row in rows]
    total = functools.reduce(jnp.add, parts)
    inverse = 1.0 / total
    return [part * inverse for part in parts], top + jnp.log2(total)


def column(row):
    lead = row.shape[:-2]
    lane = lax.broadcasted_iota(jnp.int32, lead + (16, 128), len(lead) + 1)
    sub = lax.broadcasted_iota(jnp.int32, lead + (16, 128), len(lead))
    wide = jnp.where(lane == sub, jnp.broadcast_to(row, lead + (16, 128)), 0.0)
    return jnp.sum(wide, axis=-1, keepdims=True)


def weighted(weights, parts):
    acc = None
    for weight, part in zip(weights, parts):
        term = column(weight) * part.astype(jnp.float32)
        acc = term if acc is None else acc + term
    return acc


def kernel(
    offset_hbm, lam_hbm, gain_hbm, q_ref, k_ref, v_ref, out_ref,
    offset_ref, lam_ref, gain_ref,
    kbuf, vbuf, qbuf, bias, tall, scores, expo, inverse, maps, obuf, sbuf, part, part_row,
    part_a, part_b, srow_a, srow_b, send_a, send_b, srow2_a, srow2_b, got_a, got_b, sgot_a, sgot_b,
    zsend, zsrow, zbuf, zsbuf, fin,
    small_sem, kl_sem, vl_sem, ql_sem, k_ssem, k_rsem, v_ssem, v_rsem, q_ssem, q_rsem,
    p_ssem, p_rsem, pr_ssem, pr_rsem,
    a_ssem, a_rsem, b_ssem, b_rsem, ta_ssem, ta_rsem, tb_ssem, tb_rsem,
    a2_ssem, a2_rsem, b2_ssem, b2_rsem, ta2_ssem, ta2_rsem, tb2_ssem, tb2_rsem,
    z_ssem, z_rsem, zt_ssem, zt_rsem, g_ssem, g_rsem, token_sem,
):
    ctx = lax.axis_index("ctx")
    blk = lax.axis_index("blk")
    core = lax.rem(ctx, 2)
    z = lax.rem(ctx // 2, NZ)
    y_lo = ctx // (2 * NZ)
    x = blk // 2
    y = lax.rem(blk, 2) * 2 + y_lo
    other = 1 - core
    y_hi = lax.rem(blk, 2)
    xs = [wrap(x + d, NX) for d in range(1, NX)]
    ys = [wrap(y + d, NY) for d in range(1, NY)]
    beside = (ctx + other - core, blk)
    pair = (ctx + 2 * NZ * (1 - 2 * y_lo), blk)
    ctx_of = [(lax.rem(yy, 2) * NZ + z) * 2 + core for yy in [y] + ys]
    hi_of = [yy // 2 for yy in [y] + ys]
    plane = [
        (xx, yy, (ctx_of[j], xx * 2 + hi_of[j]))
        for xx in [x] + xs
        for j, yy in enumerate([y] + ys)
    ][1:]
    x_line = [(ctx, xx * 2 + y_hi) for xx in xs]
    y_line = [(c, x * 2 + hi) for c, hi in zip(ctx_of, hi_of)][1:]
    mirror = [(pair[0], xx * 2 + 1 - y_hi) for xx in [x] + xs]
    z_base = y_lo * 2 * NZ + core

    def z_line(d):
        return (z_base + 2 * wrap(z + d, NZ), blk)

    steps = (0, other - core, 2 * NZ * (1 - 2 * y_lo), 2 * NZ * (1 - 2 * y_lo) + other - core)

    def column_at(i, zz):
        return (z_base + steps[i] + 2 * zz, blk)

    def cols(which, head, count=1):
        return pl.ds(pl.multiple_of(which * (HEADS * WIDE) + head * WIDE, WIDE), count * WIDE)

    barrier = pltpu.get_barrier_semaphore()

    def greet(to):
        pl.semaphore_signal(barrier, inc=1, device_id=to, device_id_type=MESH)

    near = [beside] + [to for _, _, to in plane] + [z_line(1), z_line(NZ - 1), column_at(3, z)]
    for to in near:
        greet(to)

    def own_copies(h):
        return (
            pltpu.make_async_copy(k_ref.at[:, cols(core, h)], kbuf.at[h, pl.ds(0, KEYS)], kl_sem.at[h]),
            pltpu.make_async_copy(v_ref.at[:, cols(core, h)], vbuf.at[h, pl.ds(0, KEYS)], vl_sem.at[h]),
        )

    def start_own(h):
        for copy in own_copies(h):
            copy.start()

    own_q = pltpu.make_async_copy(q_ref.at[:, cols(core, 0, HEADS)], qbuf.at[blk], ql_sem)
    own_q.start()
    loop(HEADS, start_own)
    small = [
        pltpu.make_async_copy(offset_hbm, offset_ref, small_sem.at[0]),
        pltpu.make_async_copy(lam_hbm, lam_ref, small_sem.at[1]),
        pltpu.make_async_copy(gain_hbm, gain_ref, small_sem.at[2]),
    ]
    for copy in small:
        copy.start()
    pl.semaphore_wait(barrier, len(near))

    def pushes(h):
        return (
            pltpu.make_async_remote_copy(
                src_ref=k_ref.at[:, cols(other, h)], dst_ref=kbuf.at[h, pl.ds(KEYS, KEYS)], send_sem=k_ssem.at[h],
                recv_sem=k_rsem.at[h], device_id=beside, device_id_type=MESH,
            ),
            pltpu.make_async_remote_copy(
                src_ref=v_ref.at[:, cols(other, h)], dst_ref=vbuf.at[h, pl.ds(KEYS, KEYS)], send_sem=v_ssem.at[h],
                recv_sem=v_rsem.at[h], device_id=beside, device_id_type=MESH,
            ),
        )

    def push(h):
        for copy in pushes(h):
            copy.start()

    def queries_of(h):
        return qbuf.at[pl.ds(0, 7), :, cols(0, h)]

    def push_head(h):
        mine = q_ref.at[:, cols(core, h)]
        for to in mirror + x_line:
            send(mine, qbuf.at[blk, :, cols(0, h)], q_ssem.at[h], q_rsem.at[h], to)
        push(h)

    loop(HEADS, push_head)

    def token(step):
        for d in (2**step, NZ - 2**step):
            pl.semaphore_signal(token_sem.at[step], inc=1, device_id=z_line(d), device_id_type=MESH)

    token(0)

    row = lax.broadcasted_iota(jnp.int32, (32 * CHUNK, KEYS), 0)
    pos = lax.broadcasted_iota(jnp.int32, (32 * CHUNK, KEYS), 1)
    ahead = pos - (lax.shift_right_logical(row, 4) * CHUNK + (row & (CHUNK - 1)))
    small[0].wait()
    for s in range(2):
        owner = ctx if s == 0 else ctx + other - core
        start = (owner * 8 + blk) * KEYS
        bias[:, s * KEYS : s * KEYS + KEYS] = jnp.where(ahead <= offset_ref[0] - start, 0.0, HIDDEN)

    scale = DH ** (-0.5) * math.log2(math.e)

    blocks = [slice(32 * b, 32 * b + 32) for b in range(8)]

    def prepare(h):
        wait_bytes(queries_of(h), q_rsem.at[h])
        lane = lax.broadcasted_iota(jnp.int32, (2, CHUNK, WIDE), 2)
        for b, rows in enumerate(blocks):
            q = qbuf[b, :, cols(0, h)].astype(jnp.float32).reshape(2, CHUNK, WIDE)
            both = jnp.concatenate([jnp.where(lane < DH, q, 0.0), jnp.where(lane >= DH, q, 0.0)], axis=1)
            tall[h % 2, rows] = both.reshape(32, WIDE).astype(jnp.bfloat16)
        own_copies(h)[0].wait()
        wait_bytes(kbuf.at[h, pl.ds(KEYS, KEYS)], k_rsem.at[h])

    def score(h, tile):
        keys = slice(256 * tile, 256 * tile + 256)
        scores[h % 2, :, keys] = lax.dot_general(
            tall[h % 2], kbuf[h, keys], (((1,), (1,)), ((), ())), preferred_element_type=jnp.float32
        )

    stat_lane = lax.broadcasted_iota(jnp.int32, (2, 16, 128), 2)
    stat_sub = lax.broadcasted_iota(jnp.int32, (2, 16, 128), 1)

    def soften(h, b):
        rows = blocks[b]
        values = scores[h % 2, rows] * scale + bias[rows]
        top = jnp.max(values, axis=1, keepdims=True)
        e = jnp.exp2(values - top)
        total = jnp.sum(e, axis=1, keepdims=True)
        expo[rows] = e.astype(jnp.bfloat16)
        inverse[rows] = jnp.broadcast_to(1.0 / total, (32, 128))
        stat = jnp.broadcast_to((top + jnp.log2(total)).reshape(2, 16, 1), (2, 16, 128))
        stat = jnp.where(stat_lane == stat_sub, stat, 0.0)
        sbuf[h, b // 2, (b % 2) * 2 : (b % 2) * 2 + 2] = jnp.sum(stat, axis=1, keepdims=True)

    def attend(h):
        own_v = own_copies(h)[1]
        if h + 1 < HEADS:
            prepare(h + 1)
        for tile, some in enumerate(((0, 1, 2), (3, 4, 5), (6, 7))):
            if h + 1 < HEADS:
                score(h + 1, tile)
            for b in some:
                soften(h, b)
        own_v.wait()
        wait_bytes(vbuf.at[h, pl.ds(KEYS, KEYS)], v_rsem.at[h])
        maps[...] = jnp.dot(expo[...], vbuf[h], preferred_element_type=jnp.float32)
        for b, rows in enumerate(blocks):
            for half in range(2):
                lanes = slice(half * DH, half * DH + DH)
                out = (maps[rows, lanes] * inverse[rows]).reshape(2, 16, DH).astype(jnp.bfloat16)
                obuf[h, b // 2, (b % 2) * 2 : (b % 2) * 2 + 2, :, lanes] = out
        if h < TWO:
            for d in range(NX - 1):
                send(sbuf.at[h, xs[d]], srow_a.at[h, d], ta_ssem.at[h], ta_rsem.at[h], x_line[d])
                send(sbuf.at[h, :, ys[d]], srow_b.at[h, d], tb_ssem.at[h], tb_rsem.at[h], y_line[d])
            for d in range(NX - 1):
                send(
                    obuf.at[h, xs[d], :, :, pl.ds(0, DH)], part_a.at[h, d],
                    a_ssem.at[h], a_rsem.at[h], x_line[d],
                )
                send(
                    obuf.at[h, :, ys[d], :, pl.ds(DH, DH)], part_b.at[h, d],
                    b_ssem.at[h], b_rsem.at[h], y_line[d],
                )
            return
        for d, (xx, yy, to) in enumerate(plane):
            send(sbuf.at[h, xx, yy], part_row.at[h - TWO, d], pr_ssem.at[h], pr_rsem.at[h], to)
            send(obuf.at[h, xx, yy], part.at[h - TWO, d], p_ssem.at[h], p_rsem.at[h], to)

    def first_step(h):
        wait_bytes(srow_a.at[h], ta_rsem.at[h])
        weights_a, whole_a = merge_rows([sbuf[h, x]] + [srow_a[h, d] for d in range(NX - 1)])
        srow2_a[h] = whole_a
        wait_bytes(srow_b.at[h], tb_rsem.at[h])
        weights_b, whole_b = merge_rows([sbuf[h, :, y]] + [srow_b[h, d] for d in range(NY - 1)])
        srow2_b[h] = whole_b
        for d in range(NX - 1):
            send(srow2_a.at[h, ys[d]], sgot_a.at[h, d], ta2_ssem.at[h], ta2_rsem.at[h], y_line[d])
            send(srow2_b.at[h, xs[d]], sgot_b.at[h, d], tb2_ssem.at[h], tb2_rsem.at[h], x_line[d])
        wait_bytes(part_a.at[h], a_rsem.at[h])
        parts = [obuf[h, x, :, :, :DH]] + [part_a[h, d] for d in range(NX - 1)]
        send_a[h] = weighted(weights_a, parts).astype(jnp.bfloat16)
        wait_bytes(part_b.at[h], b_rsem.at[h])
        parts = [obuf[h, :, y, :, DH:]] + [part_b[h, d] for d in range(NY - 1)]
        send_b[h] = weighted(weights_b, parts).astype(jnp.bfloat16)
        for d in range(NX - 1):
            send(send_a.at[h, ys[d]], got_a.at[h, d], a2_ssem.at[h], a2_rsem.at[h], y_line[d])
            send(send_b.at[h, xs[d]], got_b.at[h, d], b2_ssem.at[h], b2_rsem.at[h], x_line[d])

    def second_step(h):
        wait_bytes(sgot_a.at[h], ta2_rsem.at[h])
        wait_bytes(sgot_b.at[h], tb2_rsem.at[h])
        weights_a, whole_a = merge_rows([srow2_a[h, y]] + [sgot_a[h, d] for d in range(NY - 1)])
        weights_b, _ = merge_rows([srow2_b[h, x]] + [sgot_b[h, d] for d in range(NX - 1)])
        zsrow[h] = whole_a
        wait_bytes(got_a.at[h], a2_rsem.at[h])
        parts = [send_a[h, y]] + [got_a[h, d] for d in range(NY - 1)]
        zsend[h, :, :DH] = weighted(weights_a, parts).astype(jnp.bfloat16)
        wait_bytes(got_b.at[h], b2_rsem.at[h])
        parts = [send_b[h, x]] + [got_b[h, d] for d in range(NX - 1)]
        zsend[h, :, DH:] = weighted(weights_b, parts).astype(jnp.bfloat16)
        hand_over(h)

    def owner_of(h):
        return lax.rem(3 * h + HALF_Z - core, HALF_Z)

    def reduce(h):
        count = NX * NY - 1
        wait_bytes(part_row.at[h - TWO], pr_rsem.at[h])
        weights, whole = merge_rows([sbuf[h, x, y]] + [part_row[h - TWO, d] for d in range(count)])
        zsrow[h] = whole
        wait_bytes(part.at[h - TWO], p_rsem.at[h])
        merged = weighted(weights, [obuf[h, x, y]] + [part[h - TWO, d] for d in range(count)])
        zsend[h] = merged.astype(jnp.bfloat16)
        hand_over(h)

    def hand_over(h):
        for i in range(2):
            owner = owner_of(h) + i * HALF_Z
            gap = wrap(owner - z + NZ, NZ)

            @pl.when(gap != 0)
            def _():
                to = (z_base + 2 * owner, blk)
                send(zsrow.at[h], zsbuf.at[gap - 1], zt_ssem.at[h, i], zt_rsem, to)
                send(zsend.at[h], zbuf.at[gap - 1], z_ssem.at[h, i], z_rsem, to)

    own_q.wait()
    pl.semaphore_wait(token_sem.at[0], 2)
    token(1)
    prepare(0)
    for tile in range(3):
        score(0, tile)
    for i in range(HEADS + LAG):
        if i < HEADS:
            attend(i)
        if i == 0:
            pl.semaphore_wait(token_sem.at[1], 2)
            token(2)
        if i == LAG:
            pl.semaphore_wait(token_sem.at[2], 2)
        if LAG <= i < TWO + LAG:
            first_step(i - LAG)
        if 2 * LAG <= i < TWO + 2 * LAG:
            second_step(i - 2 * LAG)
        if TWO + LAG <= i:
            reduce(i - LAG)

    mine = lax.rem(3 * (z + core), HALF_Z)
    is_owner = mine < HEADS
    all_tiles = 4 * HEADS
    small[1].wait()
    small[2].wait()

    @pl.when(is_owner)
    def _():
        wait_bytes(zsbuf, zt_rsem)
        weights, _ = merge_rows([zsrow[mine]] + [zsbuf[d] for d in range(NZ - 1)])
        wait_bytes(zbuf, z_rsem)
        acc = weighted(weights, [zsend[mine]] + [zbuf[d] for d in range(NZ - 1)])
        head = core * HEADS + mine
        attended = acc[:CHUNK] - lam_ref[head] * acc[CHUNK:]
        spread = jnp.sqrt(jnp.mean(attended * attended, axis=-1, keepdims=True) + 1e-5)
        normed = attended / spread * gain_ref[cols(0, head)].reshape(1, WIDE)
        halves = jnp.concatenate([normed[:, :DH], normed[:, DH:]], axis=0)
        slot = (y_lo * 2 + core) * HEADS + mine
        fin[slot] = halves.astype(jnp.bfloat16)
        tile = fin.at[slot]

        def give(d):
            zz = wrap(wrap(z + d + NZ - REACH, 2 * NZ), NZ)
            for i in range(1, 4):
                send(tile, tile, g_ssem.at[i], g_rsem, column_at(i, zz))

            @pl.when(zz != z)
            def _():
                send(tile, tile, g_ssem.at[0], g_rsem, column_at(0, zz))

        loop(HALF_Z, give)
        wait_bytes(fin.at[pl.ds(0, all_tiles - 1)], g_rsem)

    @pl.when(jnp.logical_not(is_owner))
    def _():
        wait_bytes(fin, g_rsem)

    def assemble(h):
        for c in range(2):
            first = fin[c * HEADS + h].astype(jnp.float32)
            second = fin[(2 + c) * HEADS + h].astype(jnp.float32)
            low = jnp.concatenate([first[:CHUNK], second[:CHUNK]], axis=0)
            high = jnp.concatenate([first[CHUNK:], second[CHUNK:]], axis=0)
            out_ref[:, cols(c, h)] = jnp.concatenate([low, high], axis=1).astype(jnp.bfloat16)

    loop(HEADS, assemble)

    def left(h):
        for copy in pushes(h):
            copy.wait_send()
        wait_bytes(queries_of(h), q_ssem.at[h])

        for i in range(2):

            @pl.when(owner_of(h) + i * HALF_Z != z)
            def _():
                wait_bytes(zsend.at[h], z_ssem.at[h, i])
                wait_bytes(zsrow.at[h], zt_ssem.at[h, i])

    loop(HEADS, left)
    for h in range(TWO, HEADS):
        wait_bytes(part.at[h - TWO], p_ssem.at[h])
        wait_bytes(part_row.at[h - TWO], pr_ssem.at[h])
    for h in range(TWO):
        for landed, sem in (
            (part_a, a_ssem), (part_b, b_ssem), (srow_a, ta_ssem), (srow_b, tb_ssem),
            (got_a, a2_ssem), (got_b, b2_ssem), (sgot_a, ta2_ssem), (sgot_b, tb2_ssem),
        ):
            wait_bytes(landed.at[h], sem.at[h])
    @pl.when(is_owner)
    def _():
        wait_bytes(fin.at[pl.ds(0, HALF_Z - 1)], g_ssem.at[0])
        for i in range(1, 4):
            wait_bytes(fin.at[pl.ds(0, HALF_Z)], g_ssem.at[i])


def per_device(queries, keys, values, offset, lambdas, gain):
    row_count, width = queries.shape
    bf16, f32 = jnp.bfloat16, jnp.float32
    dma = pltpu.SemaphoreType.DMA
    heads = dma((HEADS,))
    hbm = pl.BlockSpec(memory_space=pltpu.HBM)
    vmem = pl.BlockSpec(memory_space=pltpu.VMEM)
    return pl.pallas_call(
        kernel,
        out_shape=jax.ShapeDtypeStruct((row_count, width), bf16),
        in_specs=[hbm] * 6,
        out_specs=vmem,
        scratch_shapes=[
            pltpu.SMEM((1,), jnp.int32),
            pltpu.SMEM(lambdas.shape, f32),
            pltpu.VMEM(gain.shape, f32),
            pltpu.VMEM((HEADS, 2 * KEYS, WIDE), bf16),
            pltpu.VMEM((HEADS, 2 * KEYS, WIDE), bf16),
            pltpu.VMEM((8, 16, HEADS * WIDE), bf16),
            pltpu.VMEM((256, 2 * KEYS), f32),
            pltpu.VMEM((2, 256, WIDE), bf16),
            pltpu.VMEM((2, 256, 2 * KEYS), f32),
            pltpu.VMEM((256, 2 * KEYS), bf16),
            pltpu.VMEM((256, 128), f32),
            pltpu.VMEM((256, WIDE), f32),
            pltpu.VMEM((HEADS, NX, NY, 16, WIDE), bf16),
            pltpu.VMEM((HEADS, NX, NY, 1, 128), f32),
            pltpu.VMEM((HEADS - TWO, NX * NY - 1, 16, WIDE), bf16),
            pltpu.VMEM((HEADS - TWO, NX * NY - 1, 1, 128), f32),
            pltpu.VMEM((TWO, NX - 1, NY, 16, DH), bf16),
            pltpu.VMEM((TWO, NY - 1, NX, 16, DH), bf16),
            pltpu.VMEM((TWO, NX - 1, NY, 1, 128), f32),
            pltpu.VMEM((TWO, NY - 1, NX, 1, 128), f32),
            pltpu.VMEM((TWO, NY, 16, DH), bf16),
            pltpu.VMEM((TWO, NX, 16, DH), bf16),
            pltpu.VMEM((TWO, NY, 1, 128), f32),
            pltpu.VMEM((TWO, NX, 1, 128), f32),
            pltpu.VMEM((TWO, NY - 1, 16, DH), bf16),
            pltpu.VMEM((TWO, NX - 1, 16, DH), bf16),
            pltpu.VMEM((TWO, NY - 1, 1, 128), f32),
            pltpu.VMEM((TWO, NX - 1, 1, 128), f32),
            pltpu.VMEM((HEADS, 16, WIDE), bf16),
            pltpu.VMEM((HEADS, 1, 128), f32),
            pltpu.VMEM((NZ - 1, 16, WIDE), bf16),
            pltpu.VMEM((NZ - 1, 1, 128), f32),
            pltpu.VMEM((4 * HEADS, 16, DH), bf16),
            dma((3,)), heads, heads, dma,
            heads, heads, heads, heads, heads, heads,
            heads, heads, heads, heads,
            heads, heads, heads, heads, heads, heads, heads, heads,
            heads, heads, heads, heads, heads, heads, heads, heads,
            dma((HEADS, 2)), dma, dma((HEADS, 2)), dma, dma((4,)), dma,
            pltpu.SemaphoreType.REGULAR((3,)),
        ],
        compiler_params=pltpu.CompilerParams(
            collective_id=0, has_side_effects=True, vmem_limit_bytes=64 * 1024 * 1024
        ),
        cost_estimate=pl.CostEstimate(flops=800_000_000, bytes_accessed=8_000_000, transcendentals=1_000_000),
    )(offset, lambdas, gain, queries, keys, values)


def solution(mesh):
    return jax.shard_map(
        per_device,
        mesh=mesh,
        in_specs=(P("blk", None), P(("ctx", "blk"), None), P(("ctx", "blk"), None), P(), P(), P()),
        out_specs=P("blk", None),
        check_vma=False,
    )
```

```python
import functools
import math

import jax
import jax.numpy as jnp
from jax import lax
from jax.experimental import pallas as pl
from jax.experimental.pallas import tpu as pltpu
from jax.sharding import PartitionSpec as P

NX, NY, NZ = 4, 4, 16
CHUNK = 8
HEADS = 5
HALF_Z = NZ // 2
REACH = 3
DH = 128
WIDE = 2 * DH
KEYS = 384
HIDDEN = -1e30
MESH = pl.DeviceIdType.MESH


LAG = 2


def wrap(index, size):
    return jnp.where(index >= size, index - size, index)


def wait_bytes(ref, sem):
    pltpu.make_async_copy(ref, ref, sem).wait()


def send(src, dst, ssem, rsem, to):
    copy = pltpu.make_async_remote_copy(
        src_ref=src, dst_ref=dst, send_sem=ssem, recv_sem=rsem, device_id=to, device_id_type=MESH
    )
    copy.start()
    return copy


def loop(count, body, start=0):
    def step(i, carry):
        body(i)
        return carry

    lax.fori_loop(start, count, step, 0)


def merge_rows(rows):
    top = functools.reduce(jnp.maximum, rows)
    parts = [jnp.exp2(row - top) for row in rows]
    total = functools.reduce(jnp.add, parts)
    inverse = 1.0 / total
    return [part * inverse for part in parts], top + jnp.log2(total)


def column(row):
    lead = row.shape[:-2]
    lane = lax.broadcasted_iota(jnp.int32, lead + (16, 128), len(lead) + 1)
    sub = lax.broadcasted_iota(jnp.int32, lead + (16, 128), len(lead))
    wide = jnp.where(lane == sub, jnp.broadcast_to(row, lead + (16, 128)), 0.0)
    return jnp.sum(wide, axis=-1, keepdims=True)


def weighted(weights, parts):
    acc = None
    for weight, part in zip(weights, parts):
        term = column(weight) * part.astype(jnp.float32)
        acc = term if acc is None else acc + term
    return acc


def kernel(
    offset_hbm, lam_hbm, gain_hbm, q_ref, k_ref, v_ref, out_ref,
    offset_ref, lam_ref, gain_ref,
    kbuf, vbuf, qbuf, bias, tall, scores, expo, inverse, maps, obuf, sbuf, part, part_row,
    zsend, zsrow, zbuf, zsbuf, fin,
    small_sem, kl_sem, vl_sem, ql_sem, k_ssem, k_rsem, v_ssem, v_rsem, q_ssem, q_rsem,
    p_ssem, p_rsem, pr_ssem, pr_rsem,
    z_ssem, z_rsem, zt_ssem, zt_rsem, g_ssem, g_rsem, token_sem,
):
    ctx = lax.axis_index("ctx")
    blk = lax.axis_index("blk")
    core = lax.rem(ctx, 2)
    z = lax.rem(ctx // 2, NZ)
    y_lo = ctx // (2 * NZ)
    x = blk // 2
    y = lax.rem(blk, 2) * 2 + y_lo
    other = 1 - core
    y_hi = lax.rem(blk, 2)
    xs = [wrap(x + d, NX) for d in range(1, NX)]
    ys = [wrap(y + d, NY) for d in range(1, NY)]
    beside = (ctx + other - core, blk)
    pair = (ctx + 2 * NZ * (1 - 2 * y_lo), blk)
    ctx_of = [(lax.rem(yy, 2) * NZ + z) * 2 + core for yy in [y] + ys]
    hi_of = [yy // 2 for yy in [y] + ys]
    plane = [
        (xx, yy, (ctx_of[j], xx * 2 + hi_of[j]))
        for xx in [x] + xs
        for j, yy in enumerate([y] + ys)
    ][1:]
    hops = (0, 1, 2, 1)
    far_first = sorted(range(NX * NY - 1), key=lambda d: -hops[(d + 1) // NY] - hops[(d + 1) % NY])
    x_line = [(ctx, xx * 2 + y_hi) for xx in xs]
    mirror = [(pair[0], xx * 2 + 1 - y_hi) for xx in [x] + xs]
    z_base = y_lo * 2 * NZ + core

    def z_line(d):
        return (z_base + 2 * wrap(z + d, NZ), blk)

    steps = (0, other - core, 2 * NZ * (1 - 2 * y_lo), 2 * NZ * (1 - 2 * y_lo) + other - core)

    def column_at(i, zz):
        return (z_base + steps[i] + 2 * zz, blk)

    def cols(which, head, count=1):
        return pl.ds(pl.multiple_of(which * (HEADS * WIDE) + head * WIDE, WIDE), count * WIDE)

    barrier = pltpu.get_barrier_semaphore()

    def greet(to):
        pl.semaphore_signal(barrier, inc=1, device_id=to, device_id_type=MESH)

    near = [beside] + [to for _, _, to in plane] + [z_line(1), z_line(NZ - 1), column_at(3, z)]
    for to in near:
        greet(to)

    def own_copies(h):
        return (
            pltpu.make_async_copy(k_ref.at[:, cols(core, h)], kbuf.at[h, pl.ds(0, KEYS)], kl_sem.at[h]),
            pltpu.make_async_copy(v_ref.at[:, cols(core, h)], vbuf.at[h, pl.ds(0, KEYS)], vl_sem.at[h]),
        )

    def start_own(h):
        for copy in own_copies(h):
            copy.start()

    own_q = pltpu.make_async_copy(q_ref.at[:, cols(core, 0, HEADS)], qbuf.at[blk], ql_sem)
    own_q.start()
    loop(HEADS, start_own)
    small = [
        pltpu.make_async_copy(offset_hbm, offset_ref, small_sem.at[0]),
        pltpu.make_async_copy(lam_hbm, lam_ref, small_sem.at[1]),
        pltpu.make_async_copy(gain_hbm, gain_ref, small_sem.at[2]),
    ]
    for copy in small:
        copy.start()
    pl.semaphore_wait(barrier, len(near))

    def pushes(h):
        return (
            pltpu.make_async_remote_copy(
                src_ref=k_ref.at[:, cols(other, h)], dst_ref=kbuf.at[h, pl.ds(KEYS, KEYS)], send_sem=k_ssem.at[h],
                recv_sem=k_rsem.at[h], device_id=beside, device_id_type=MESH,
            ),
            pltpu.make_async_remote_copy(
                src_ref=v_ref.at[:, cols(other, h)], dst_ref=vbuf.at[h, pl.ds(KEYS, KEYS)], send_sem=v_ssem.at[h],
                recv_sem=v_rsem.at[h], device_id=beside, device_id_type=MESH,
            ),
        )

    def push(h):
        for copy in pushes(h):
            copy.start()

    def queries_of(h):
        return qbuf.at[pl.ds(0, 7), :, cols(0, h)]

    def push_head(h):
        mine = q_ref.at[:, cols(core, h)]
        for to in (mirror[2], x_line[1], mirror[1], mirror[3], x_line[0], x_line[2], mirror[0]):
            send(mine, qbuf.at[blk, :, cols(0, h)], q_ssem.at[h], q_rsem.at[h], to)
        push(h)

    loop(HEADS, push_head)

    def token(step):
        for d in (2**step, NZ - 2**step):
            pl.semaphore_signal(token_sem.at[step], inc=1, device_id=z_line(d), device_id_type=MESH)

    token(0)

    row = lax.broadcasted_iota(jnp.int32, (32 * CHUNK, KEYS), 0)
    pos = lax.broadcasted_iota(jnp.int32, (32 * CHUNK, KEYS), 1)
    ahead = pos - (lax.shift_right_logical(row, 4) * CHUNK + (row & (CHUNK - 1)))
    small[0].wait()
    for s in range(2):
        owner = ctx if s == 0 else ctx + other - core
        start = (owner * 8 + blk) * KEYS
        bias[:, s * KEYS : s * KEYS + KEYS] = jnp.where(ahead <= offset_ref[0] - start, 0.0, HIDDEN)

    scale = DH ** (-0.5) * math.log2(math.e)

    def attend(h):
        own_k, own_v = own_copies(h)
        wait_bytes(queries_of(h), q_rsem.at[h])
        blocks = [slice(32 * b, 32 * b + 32) for b in range(8)]
        lane = lax.broadcasted_iota(jnp.int32, (2, CHUNK, WIDE), 2)
        for b, rows in enumerate(blocks):
            q = qbuf[b, :, cols(0, h)].astype(jnp.float32).reshape(2, CHUNK, WIDE)
            both = jnp.concatenate([jnp.where(lane < DH, q, 0.0), jnp.where(lane >= DH, q, 0.0)], axis=1)
            tall[rows] = both.reshape(32, WIDE).astype(jnp.bfloat16)
        own_k.wait()
        wait_bytes(kbuf.at[h, pl.ds(KEYS, KEYS)], k_rsem.at[h])
        scores[...] = lax.dot_general(
            tall[...], kbuf[h], (((1,), (1,)), ((), ())), preferred_element_type=jnp.float32
        )
        stat_lane = lax.broadcasted_iota(jnp.int32, (2, 16, 128), 2)
        stat_sub = lax.broadcasted_iota(jnp.int32, (2, 16, 128), 1)
        for b, rows in enumerate(blocks):
            score = scores[rows] * scale + bias[rows]
            top = jnp.max(score, axis=1, keepdims=True)
            e = jnp.exp2(score - top)
            total = jnp.sum(e, axis=1, keepdims=True)
            expo[rows] = e.astype(jnp.bfloat16)
            inverse[rows] = jnp.broadcast_to(1.0 / total, (32, 128))
            stat = jnp.broadcast_to((top + jnp.log2(total)).reshape(2, 16, 1), (2, 16, 128))
            stat = jnp.where(stat_lane == stat_sub, stat, 0.0)
            sbuf[h, b // 2, (b % 2) * 2 : (b % 2) * 2 + 2] = jnp.sum(stat, axis=1, keepdims=True)
        own_v.wait()
        wait_bytes(vbuf.at[h, pl.ds(KEYS, KEYS)], v_rsem.at[h])
        maps[...] = jnp.dot(expo[...], vbuf[h], preferred_element_type=jnp.float32)
        for b, rows in enumerate(blocks):
            for half in range(2):
                lanes = slice(half * DH, half * DH + DH)
                out = (maps[rows, lanes] * inverse[rows]).reshape(2, 16, DH).astype(jnp.bfloat16)
                obuf[h, b // 2, (b % 2) * 2 : (b % 2) * 2 + 2, :, lanes] = out
        for d in far_first:
            xx, yy, to = plane[d]
            send(sbuf.at[h, xx, yy], part_row.at[h, d], pr_ssem.at[h], pr_rsem.at[h], to)
            send(obuf.at[h, xx, yy], part.at[h, d], p_ssem.at[h], p_rsem.at[h], to)

    def owner_of(h):
        return lax.rem(3 * h + HALF_Z - core, HALF_Z)

    def reduce(h):
        count = NX * NY - 1
        wait_bytes(part_row.at[h], pr_rsem.at[h])
        weights, whole = merge_rows([sbuf[h, x, y]] + [part_row[h, d] for d in range(count)])
        zsrow[h] = whole
        wait_bytes(part.at[h], p_rsem.at[h])
        merged = weighted(weights, [obuf[h, x, y]] + [part[h, d] for d in range(count)])
        zsend[h] = merged.astype(jnp.bfloat16)
        for i in range(2):
            owner = owner_of(h) + i * HALF_Z
            gap = wrap(owner - z + NZ, NZ)

            @pl.when(gap != 0)
            def _():
                to = (z_base + 2 * owner, blk)
                send(zsrow.at[h], zsbuf.at[gap - 1], zt_ssem.at[h, i], zt_rsem, to)
                send(zsend.at[h], zbuf.at[gap - 1], z_ssem.at[h, i], z_rsem, to)

    def turn_of(i):
        @pl.when(i < HEADS)
        def _():
            attend(i)

        @pl.when(i == 0)
        def _():
            pl.semaphore_wait(token_sem.at[1], 2)
            token(2)

        @pl.when(i == LAG)
        def _():
            pl.semaphore_wait(token_sem.at[2], 2)

        @pl.when(i >= LAG)
        def _():
            reduce(i - LAG)

    own_q.wait()
    pl.semaphore_wait(token_sem.at[0], 2)
    token(1)
    loop(HEADS + LAG, turn_of)

    def left(h):
        for copy in pushes(h):
            copy.wait_send()
        wait_bytes(queries_of(h), q_ssem.at[h])
        wait_bytes(part.at[h], p_ssem.at[h])
        wait_bytes(part_row.at[h], pr_ssem.at[h])

        for i in range(2):

            @pl.when(owner_of(h) + i * HALF_Z != z)
            def _():
                wait_bytes(zsend.at[h], z_ssem.at[h, i])
                wait_bytes(zsrow.at[h], zt_ssem.at[h, i])

    loop(HEADS, left)
    mine = lax.rem(3 * (z + core), HALF_Z)
    is_owner = mine < HEADS
    all_tiles = 4 * HEADS
    small[1].wait()
    small[2].wait()

    @pl.when(is_owner)
    def _():
        wait_bytes(zsbuf, zt_rsem)
        weights, _ = merge_rows([zsrow[mine]] + [zsbuf[d] for d in range(NZ - 1)])
        wait_bytes(zbuf, z_rsem)
        acc = weighted(weights, [zsend[mine]] + [zbuf[d] for d in range(NZ - 1)])
        head = core * HEADS + mine
        attended = acc[:CHUNK] - lam_ref[head] * acc[CHUNK:]
        spread = jnp.sqrt(jnp.mean(attended * attended, axis=-1, keepdims=True) + 1e-5)
        normed = attended / spread * gain_ref[cols(0, head)].reshape(1, WIDE)
        halves = jnp.concatenate([normed[:, :DH], normed[:, DH:]], axis=0)
        slot = (y_lo * 2 + core) * HEADS + mine
        fin[slot] = halves.astype(jnp.bfloat16)
        tile = fin.at[slot]

        def give(d):
            zz = wrap(wrap(z + d + NZ - REACH, 2 * NZ), NZ)
            for i in range(1, 4):
                send(tile, tile, g_ssem.at[i], g_rsem, column_at(i, zz))

            @pl.when(zz != z)
            def _():
                send(tile, tile, g_ssem.at[0], g_rsem, column_at(0, zz))

        loop(HALF_Z, give)
        wait_bytes(fin.at[pl.ds(0, all_tiles - 1)], g_rsem)

    @pl.when(jnp.logical_not(is_owner))
    def _():
        wait_bytes(fin, g_rsem)

    def assemble(h):
        for c in range(2):
            first = fin[c * HEADS + h].astype(jnp.float32)
            second = fin[(2 + c) * HEADS + h].astype(jnp.float32)
            low = jnp.concatenate([first[:CHUNK], second[:CHUNK]], axis=0)
            high = jnp.concatenate([first[CHUNK:], second[CHUNK:]], axis=0)
            out_ref[:, cols(c, h)] = jnp.concatenate([low, high], axis=1).astype(jnp.bfloat16)

    loop(HEADS, assemble)

    @pl.when(is_owner)
    def _():
        wait_bytes(fin.at[pl.ds(0, HALF_Z - 1)], g_ssem.at[0])
        for i in range(1, 4):
            wait_bytes(fin.at[pl.ds(0, HALF_Z)], g_ssem.at[i])


def per_device(queries, keys, values, offset, lambdas, gain):
    row_count, width = queries.shape
    bf16, f32 = jnp.bfloat16, jnp.float32
    dma = pltpu.SemaphoreType.DMA
    heads = dma((HEADS,))
    hbm = pl.BlockSpec(memory_space=pltpu.HBM)
    vmem = pl.BlockSpec(memory_space=pltpu.VMEM)
    return pl.pallas_call(
        kernel,
        out_shape=jax.ShapeDtypeStruct((row_count, width), bf16),
        in_specs=[hbm] * 6,
        out_specs=vmem,
        scratch_shapes=[
            pltpu.SMEM((1,), jnp.int32),
            pltpu.SMEM(lambdas.shape, f32),
            pltpu.VMEM(gain.shape, f32),
            pltpu.VMEM((HEADS, 2 * KEYS, WIDE), bf16),
            pltpu.VMEM((HEADS, 2 * KEYS, WIDE), bf16),
            pltpu.VMEM((8, 16, HEADS * WIDE), bf16),
            pltpu.VMEM((256, 2 * KEYS), f32),
            pltpu.VMEM((256, WIDE), bf16),
            pltpu.VMEM((256, 2 * KEYS), f32),
            pltpu.VMEM((256, 2 * KEYS), bf16),
            pltpu.VMEM((256, 128), f32),
            pltpu.VMEM((256, WIDE), f32),
            pltpu.VMEM((HEADS, NX, NY, 16, WIDE), bf16),
            pltpu.VMEM((HEADS, NX, NY, 1, 128), f32),
            pltpu.VMEM((HEADS, NX * NY - 1, 16, WIDE), bf16),
            pltpu.VMEM((HEADS, NX * NY - 1, 1, 128), f32),
            pltpu.VMEM((HEADS, 16, WIDE), bf16),
            pltpu.VMEM((HEADS, 1, 128), f32),
            pltpu.VMEM((NZ - 1, 16, WIDE), bf16),
            pltpu.VMEM((NZ - 1, 1, 128), f32),
            pltpu.VMEM((4 * HEADS, 16, DH), bf16),
            dma((3,)), heads, heads, dma,
            heads, heads, heads, heads, heads, heads,
            heads, heads, heads, heads,
            dma((HEADS, 2)), dma, dma((HEADS, 2)), dma, dma((4,)), dma,
            pltpu.SemaphoreType.REGULAR((3,)),
        ],
        compiler_params=pltpu.CompilerParams(
            collective_id=0, has_side_effects=True, vmem_limit_bytes=64 * 1024 * 1024
        ),
        cost_estimate=pl.CostEstimate(flops=800_000_000, bytes_accessed=8_000_000, transcendentals=1_000_000),
    )(offset, lambdas, gain, queries, keys, values)


def solution(mesh):
    return jax.shard_map(
        per_device,
        mesh=mesh,
        in_specs=(P("blk", None), P(("ctx", "blk"), None), P(("ctx", "blk"), None), P(), P(), P()),
        out_specs=P("blk", None),
        check_vma=False,
    )
```
